128 devices in a mesh: cell: 16 (over y, x), station: 8 (over z, core).
Axes of the slice: x: 4, y: 4, z: 4, core: 2. Of those that a mesh axis runs over, the one named last changes fastest.
Arguments:
- sensitivity: float32 [2048, 262144], P('station', 'cell'), may hold values from -6 to 6
- tile_mask: int32 [16, 512], P('station', 'cell'), may hold values 0 or 1
- data_panel: float32 [32, 2048], P('cell', 'station'), may hold values from -6 to 6
- model_panel: float32 [32, 262144], P('station', 'cell'), may hold values from -6 to 6
Outputs:
- data_vector: float32 [2048], P('station')
- model_vector: float32 [262144], P('cell')
- bidiag: float32 [4], replicated
The draws below stay inside these ranges and needn't reach their ends.
All inputs are finite; a program needn't handle non-finite values. No bound on the sum of `tile_mask` on one device may be relied on, other than what follows from the above.
Results may differ from the reference program's by a relative error of at most 0.0003.
Values sent between devices are 32-bit elements; how exact they have to be, the bound alone decides.
A program may use at most 128 MiB of HBM per device.

```python
import math
import jax
import jax.numpy as jnp
from jax import lax

KRYLOV = 32
TILE_ROWS = 128
TILE_COLS = 512
DATA = 2048
CELLS = 262144


def place_ends(drawn, own_key, low, top_value):
    longest = drawn.shape.index(max(drawn.shape))
    spots = []
    for shift in (0, 1):
        where = [jax.random.randint(jax.random.fold_in(own_key, axis), (), 0, length) for axis, length in enumerate(drawn.shape)]
        where[longest] = (where[longest] + shift) % drawn.shape[longest]
        spots.append(tuple(where))
    return drawn.at[spots[0]].set(low).at[spots[1]].set(top_value)


def block_levels(stream_key, shape, cuts, low, top_value):
    gain, own = 1.0, jax.random.fold_in(stream_key, 6)
    for position, blocks in cuts:
        steps = jnp.exp(jax.random.uniform(jax.random.fold_in(own, position), (blocks,), jnp.float32, low / len(cuts), top_value / len(cuts)))
        gain = gain * jnp.repeat(steps, shape[position] // blocks).reshape([-1 if axis == position else 1 for axis in range(len(shape))])
    return gain


def normal_values(key, shape, spread, most, cuts=(), held_as=jnp.bfloat16):
    result = spread * jax.random.normal(key, shape, jnp.float32)
    if cuts:
        result = result * block_levels(key, shape, cuts, -0.22, 0.18)
    return jnp.clip(result, -most, most).astype(held_as)


def setup_inputs(seed: int = 0) -> dict:
    keys = jax.random.split(jax.random.key(seed), 5)
    sensitivity = normal_values(keys[0], (DATA, CELLS), 1.0, 6.0, ((0, 8), (1, 16)), jnp.float32)
    tile_mask = place_ends((jax.random.randint(keys[1], (DATA // TILE_ROWS, CELLS // TILE_COLS), 0, 4) < 3).astype(jnp.int32), jax.random.fold_in(keys[1], 1), 0, 1)
    data_panel = normal_values(keys[2], (KRYLOV, DATA), 1.0, 6.0, ((0, 16), (1, 8)), jnp.float32)
    model_panel = normal_values(keys[3], (KRYLOV, CELLS), 1.0, 6.0, ((0, 8), (1, 16)), jnp.float32)
    return {"sensitivity": sensitivity, "tile_mask": tile_mask, "data_panel": data_panel, "model_panel": model_panel}


HIGH = lax.Precision.HIGHEST

def orthonormal(panel):
    gram = jnp.dot(panel, panel.T, precision=HIGH)
    lower = jnp.linalg.cholesky(gram)
    return lax.linalg.triangular_solve(lower, panel, left_side=True, lower=True)

def project(vector, basis):
    coef = jnp.dot(basis, vector, precision=HIGH)
    rest = vector - jnp.dot(coef, basis, precision=HIGH)
    norm = jnp.sqrt(jnp.sum(rest * rest))
    return (rest / norm, norm)

def reference(sensitivity, tile_mask, data_panel, model_panel):
    row_tiles = DATA // TILE_ROWS
    blocks = sensitivity.reshape(row_tiles, TILE_ROWS, CELLS)
    spread_mask = jnp.repeat(tile_mask.astype(jnp.float32), TILE_COLS, axis=1)

    def forward(vector):

        def one(item):
            return jnp.dot(item[0] * item[1][None, :], vector, precision=HIGH)
        return lax.map(one, (blocks, spread_mask)).reshape(DATA)

    def adjoint(vector):
        pieces = vector.reshape(row_tiles, TILE_ROWS)

        def one(item):
            return jnp.dot(item[2], item[0] * item[1][None, :], precision=HIGH)
        return lax.optimization_barrier(jnp.sum(lax.map(one, (blocks, spread_mask, pieces)), axis=0))
    basis_u = orthonormal(data_panel)
    basis_v = orthonormal(model_panel)
    start = basis_u[-1]
    first_v, alpha_one = project(adjoint(start), basis_v)
    first_u, beta_one = project(forward(first_v), basis_u)
    second_v, alpha_two = project(adjoint(first_u), jnp.concatenate([basis_v, first_v[None, :]], axis=0))
    second_u, beta_two = project(forward(second_v), jnp.concatenate([basis_u, first_u[None, :]], axis=0))
    bidiag = jnp.stack([alpha_one / math.sqrt(CELLS), beta_one / math.sqrt(DATA), alpha_two / math.sqrt(CELLS), beta_two / math.sqrt(DATA)]).astype(jnp.float32)
    return (second_u * math.sqrt(DATA), second_v * math.sqrt(CELLS), bidiag)
```

```python
import functools
import math

import jax
import jax.numpy as jnp
from jax import lax
from jax.experimental import pallas as pl
from jax.experimental.pallas import tpu as pltpu
from jax.sharding import PartitionSpec as P

TILE_ROWS = 128
TILE_COLS = 512
LANES = 128
HIGH = lax.Precision.HIGHEST
MESH = pl.DeviceIdType.MESH
F32 = jnp.float32


def eye_mask(rows):
    return lax.broadcasted_iota(jnp.int32, (rows, LANES), 0) == lax.broadcasted_iota(jnp.int32, (rows, LANES), 1)


def to_lanes(column, rows):
    return jnp.sum(jnp.where(eye_mask(rows), column, 0.0), axis=0, keepdims=True)


def to_rows(row, rows):
    return jnp.sum(jnp.where(eye_mask(rows), row, 0.0), axis=1, keepdims=True)


def lane(row, index):
    ids = lax.broadcasted_iota(jnp.int32, (1, LANES), 1)
    return jnp.sum(jnp.where(ids == index, row, 0.0), axis=1, keepdims=True)


def put_lane(row, index, value):
    ids = lax.broadcasted_iota(jnp.int32, (1, LANES), 1)
    return jnp.where(ids == index, value, row)


def total(x):
    return jnp.sum(jnp.sum(x, axis=0, keepdims=True), axis=1, keepdims=True)


def dot_t(a, b):
    return lax.dot_general(a, b, (((1,), (1,)), ((), ())), precision=HIGH, preferred_element_type=F32)


def pack(gram):
    rows = gram.shape[0] // 4
    return jnp.concatenate([gram[q * rows : (q + 1) * rows, :] for q in range(4)], axis=1)


def unpack(packed, size):
    return jnp.concatenate([packed[:, q * size : (q + 1) * size] for q in range(4)], axis=0)


def inverse(gram, size):
    rows = lax.broadcasted_iota(jnp.int32, (size, LANES), 0)
    unit = jnp.where(
        rows + size == lax.broadcasted_iota(jnp.int32, (size, LANES), 1), 1.0, 0.0
    )
    a = jnp.concatenate([gram, jnp.zeros((size, LANES - size), F32)], axis=1) + unit
    for i in range(size):
        pivot_row = a[i : i + 1, :] / a[i : i + 1, i : i + 1]
        a = jnp.where(rows == i, pivot_row, a - a[:, i : i + 1] * pivot_row)
    return jnp.concatenate([a[:, size : 2 * size], jnp.zeros((size, LANES - size), F32)], axis=1)


def kernel(
    nc, ns, total_rows, total_cols,
    sens, mask, dp, mp,
    out_u, out_v, out_b,
    g, pfull, pown, plocal, d1, p64, gu, gmc, gms,
    wpart, rs, ag, cc, cs, rbuf, fx, us, last, ub, stack, ybuf,
    load_sem, send, recv, zrecv, relay_sem, bulk_send,
):
    me_c, me_s = lax.axis_index("cell"), lax.axis_index("station")
    nz = ns // 2
    z, core = me_s // 2, me_s % 2
    partner = z * 2 + (1 - core)
    rows, cols = sens.shape
    tiles = cols // LANES
    own = tiles // ns
    kd, km = dp.shape[0], mp.shape[0]
    size = kd * nc
    halves = rows // LANES
    per = TILE_COLS // LANES

    load_rows = rows // 8
    loads = [
        pltpu.make_async_copy(
            sens.at[pl.ds(q * load_rows, load_rows), :], g.at[pl.ds(q * load_rows, load_rows), :], load_sem.at[q]
        )
        for q in range(8)
    ]
    load_panel = pltpu.make_async_copy(mp, plocal, load_sem.at[8])
    load_panel.start()
    for copy in loads:
        copy.start()

    barrier = pltpu.get_barrier_semaphore()
    for d in range(1, nc):
        pl.semaphore_signal(barrier, inc=1, device_id={"cell": (me_c + d) % nc}, device_id_type=MESH)
    for d in range(1, ns):
        pl.semaphore_signal(barrier, inc=1, device_id={"station": (me_s + d) % ns}, device_id_type=MESH)

    drains = []

    def exchange(axis, src, dst, index):
        n, me = (nc, me_c) if axis == "cell" else (ns, me_s)
        for d in range(1, n):
            peer = (me + d) % n
            pltpu.make_async_remote_copy(
                src_ref=src(peer), dst_ref=dst, send_sem=send.at[index], recv_sem=recv.at[index],
                device_id={axis: peer}, device_id_type=MESH,
            ).start()

    def settle(index, span):
        pltpu.make_async_copy(span, span, recv.at[index]).wait()
        drains.append((index, span))

    block = dp[...]
    for h in range(halves):
        d1[me_c, h * kd : (h + 1) * kd, :] = block[:, h * LANES : (h + 1) * LANES]

    load_panel.wait()

    @pl.loop(0, tiles)
    def _(j):
        piece = plocal[:, pl.ds(pl.multiple_of(j * LANES, LANES), LANES)]
        for k in range(km):
            pfull[me_s * km + k, pl.ds(j, 1), :] = piece[k : k + 1, :]

    pl.semaphore_wait(barrier, nc + ns - 2)

    exchange("cell", lambda peer: d1.at[me_c], d1.at[me_c], 0)
    mine = pl.ds(me_s * km, km)
    exchange(
        "station",
        lambda peer: pfull.at[mine, pl.ds(pl.multiple_of(peer * own, own), own), :],
        pown.at[mine, :, :],
        1,
    )
    bulk = []
    for d in range(1, nz):
        copy = pltpu.make_async_remote_copy(
            src_ref=pfull.at[mine], dst_ref=pfull.at[mine], send_sem=bulk_send.at[d], recv_sem=zrecv.at[d],
            device_id={"station": ((z + d) % nz) * 2 + core}, device_id_type=MESH,
        )
        copy.start()
        bulk.append(copy)
    copy = pltpu.make_async_remote_copy(
        src_ref=pfull.at[mine], dst_ref=pfull.at[mine], send_sem=bulk_send.at[0], recv_sem=zrecv.at[0],
        device_id={"station": partner}, device_id_type=MESH,
    )
    copy.start()
    bulk.insert(0, copy)
    pown[mine, :, :] = pfull[mine, pl.ds(pl.multiple_of(me_s * own, own), own), :]

    settle(0, d1.at[pl.ds(0, nc - 1)])
    for c in range(nc):
        for h in range(halves):
            p64[h, c * kd : (c + 1) * kd, :] = d1[c, h * kd : (h + 1) * kd, :]
    gram = dot_t(p64[0], p64[0])
    for h in range(1, halves):
        gram = gram + dot_t(p64[h], p64[h])
    gu[me_s] = pack(gram)
    exchange("station", lambda peer: gu.at[me_s], gu.at[me_s], 2)

    settle(1, pown.at[pl.ds(0, km * (ns - 1))])
    mine_all = jnp.concatenate([pown[:, j, :] for j in range(own)], axis=1)
    gmc[me_c] = pack(dot_t(mine_all, mine_all))
    exchange("cell", lambda peer: gmc.at[me_c], gmc.at[me_c], 3)

    settle(2, gu.at[pl.ds(0, ns - 1)])
    t_u = inverse(unpack(jnp.sum(gu[...], axis=0), size), size)
    x_col = t_u[:, size - 1 : size] / jnp.sqrt(t_u[size - 1 : size, size - 1 : size])
    start = [jnp.sum(x_col * p64[h], axis=0, keepdims=True) for h in range(halves)]

    settle(3, gmc.at[pl.ds(0, nc - 1)])
    gms[me_s] = jnp.sum(gmc[...], axis=0)
    exchange("station", lambda peer: gms.at[me_s], gms.at[me_s], 4)

    for copy in loads:
        copy.wait()

    def adjoint(vector, t):
        for h in range(halves):
            ub[h * LANES : (h + 1) * LANES, :] = jnp.broadcast_to(to_rows(vector[h], LANES), (LANES, LANES))

        @pl.loop(0, tiles // per)
        def _(j):
            for q in range(per):
                at = pl.ds(pl.multiple_of((j * per + q) * LANES, LANES), LANES)
                result = None
                for h in range(halves):
                    parts = [None, None]
                    for r in range(h * LANES, (h + 1) * LANES, 8):
                        term = g[r : r + 8, at] * ub[r : r + 8, :]
                        w = (r // 8) % 2
                        parts[w] = term if parts[w] is None else parts[w] + term
                    part = (parts[0] + parts[1]) * mask[h, j].astype(F32)
                    result = part if result is None else result + part
                wpart[t, pl.ds(j * per + q, 1), :] = jnp.sum(result, axis=0, keepdims=True)

    def forward(t):
        def step(j, sums):
            sums = list(sums)
            for q in range(per):
                at = pl.ds(pl.multiple_of((j * per + q) * LANES, LANES), LANES)
                row = rbuf[t, pl.ds(j * per + q, 1), :]
                for h in range(halves):
                    sums[h] = sums[h] + g[h * LANES : (h + 1) * LANES, at] * (row * mask[h, j].astype(F32))
            return tuple(sums)

        sums = lax.fori_loop(0, tiles // per, step, tuple(jnp.zeros((LANES, LANES), F32) for _ in range(halves)))
        return [to_lanes(jnp.sum(part, axis=1, keepdims=True), LANES) for part in sums]

    def scatter(t, index):
        own_at = pl.ds(pl.multiple_of(me_s * own, own), own)
        rs[t, me_s] = wpart[t, own_at, :]
        exchange(
            "station",
            lambda peer: wpart.at[t, pl.ds(pl.multiple_of(peer * own, own), own), :],
            rs.at[t, me_s],
            index,
        )

    def gather(t, index_rs, index_ag):
        settle(index_rs, rs.at[t, pl.ds(0, ns - 1)])
        own_at = pl.ds(pl.multiple_of(me_s * own, own), own)
        w_own = jnp.sum(rs[t], axis=0)
        ag[t, own_at, :] = w_own
        exchange("station", lambda peer: ag.at[t, own_at, :], ag.at[t, own_at, :], index_ag)
        return w_own

    def reorthogonalise(t, w, coef, extra):
        y = jnp.sum(t_m * coef, axis=1, keepdims=True)
        ybuf[...] = jnp.broadcast_to(y, (size, LANES))
        rest = w if extra is None else w - extra

        def step(k, rest):
            return rest - pfull[k] * ybuf[pl.ds(k, 1), :]

        rest = lax.fori_loop(0, size, step, rest)
        rbuf[t] = rest
        return total(rest * rest)

    def data_side(t, index_fx, index_us, squares, before):
        parts = forward(t)
        for h in range(halves):
            fx[t, me_c, h : h + 1, :] = parts[h]
        fx[t, me_c, halves : halves + 1, :] = jnp.broadcast_to(squares, (1, LANES))
        fx[t, me_c, halves + 1 : halves + 2, :] = jnp.zeros((1, LANES), F32)
        exchange("cell", lambda peer: fx.at[t, me_c], fx.at[t, me_c], index_fx)
        settle(index_fx, fx.at[t, pl.ds(0, nc - 1)])
        summed = jnp.sum(fx[t], axis=0)
        norm = jnp.sqrt(summed[halves : halves + 1, 0:1])
        scale = 1.0 / norm
        vec = [summed[h : h + 1, :] * scale for h in range(halves)]
        col = p64[0] * vec[0]
        for h in range(1, halves):
            col = col + p64[h] * vec[h]
        coef = to_lanes(jnp.sum(col, axis=1, keepdims=True), size)
        if before is not None:
            along = sum(jnp.sum(before[h] * vec[h], axis=1, keepdims=True) for h in range(halves))
            coef = put_lane(coef, size, along)
        us[t, me_s] = coef
        exchange("station", lambda peer: us.at[t, me_s], us.at[t, me_s], index_us)
        settle(index_us, us.at[t, pl.ds(0, ns - 1)])
        coef = jnp.sum(us[t], axis=0)
        y = jnp.sum(t_u * coef, axis=1, keepdims=True)
        rest = [vec[h] - jnp.sum(y * p64[h], axis=0, keepdims=True) for h in range(halves)]
        if before is not None:
            along = lane(coef, size)
            rest = [rest[h] - along * before[h] for h in range(halves)]
        return rest, norm, scale

    def sum_squares(vector):
        return sum(jnp.sum(part * part, axis=1, keepdims=True) for part in vector)

    adjoint(start, 0)
    scatter(0, 5)
    w_own = gather(0, 5, 6)
    for k in range(size):
        stack[k : k + 1, :] = jnp.sum(pown[k] * w_own, axis=0, keepdims=True)
    cc[0, me_c] = to_lanes(jnp.sum(stack[0:size, :], axis=1, keepdims=True), size)
    exchange("cell", lambda peer: cc.at[0, me_c], cc.at[0, me_c], 7)
    settle(4, gms.at[pl.ds(0, ns - 1)])
    t_m = inverse(unpack(jnp.sum(gms[...], axis=0), size), size)
    for d in range(1, nz):
        bulk[d].wait_recv()
        theirs = pl.ds((((z + nz - d) % nz) * 2 + core) * km, km)
        copy = pltpu.make_async_remote_copy(
            src_ref=pfull.at[theirs], dst_ref=pfull.at[theirs], send_sem=relay_sem.at[0], recv_sem=relay_sem.at[1],
            device_id={"station": partner}, device_id_type=MESH,
        )
        copy.start()
    settle(7, cc.at[0, pl.ds(0, nc - 1)])
    cs[0, me_s] = jnp.sum(cc[0], axis=0)
    exchange("station", lambda peer: cs.at[0, me_s], cs.at[0, me_s], 8)
    bulk[0].wait_recv()
    relayed = pfull.at[pl.ds(0, km * (nz - 1))]
    pltpu.make_async_copy(relayed, relayed, relay_sem.at[1]).wait()
    settle(6, ag.at[0, pl.ds(0, own * (ns - 1)), :])
    settle(8, cs.at[0, pl.ds(0, ns - 1)])
    squares = reorthogonalise(0, ag[0], jnp.sum(cs[0], axis=0), None)
    rest_u, norm_v1, scale_v1 = data_side(0, 9, 10, squares, None)

    adjoint(rest_u, 1)
    scatter(1, 11)
    part = wpart[1]

    def step(k, carry):
        stack[pl.ds(k, 1), :] = jnp.sum(pfull[k] * part, axis=0, keepdims=True)
        return carry

    lax.fori_loop(0, size, step, 0)
    coef = to_lanes(jnp.sum(stack[0:size, :], axis=1, keepdims=True), size)
    coef = put_lane(coef, size, total(rbuf[0] * part) * scale_v1)
    cc[1, me_c] = coef
    exchange("cell", lambda peer: cc.at[1, me_c], cc.at[1, me_c], 12)
    gather(1, 11, 13)
    settle(12, cc.at[1, pl.ds(0, nc - 1)])
    cs[1, me_s] = put_lane(jnp.sum(cc[1], axis=0), size + 1, sum_squares(rest_u))
    exchange("station", lambda peer: cs.at[1, me_s], cs.at[1, me_s], 14)
    settle(13, ag.at[1, pl.ds(0, own * (ns - 1)), :])
    settle(14, cs.at[1, pl.ds(0, ns - 1)])
    coef = jnp.sum(cs[1], axis=0)
    norm_u1 = jnp.sqrt(lane(coef, size + 1))
    scale_u1 = 1.0 / norm_u1
    coef = coef * scale_u1
    along = rbuf[0] * (lane(coef, size) * scale_v1)
    squares = reorthogonalise(1, ag[1] * scale_u1, coef, along)
    first_u = [rest_u[h] * scale_u1 for h in range(halves)]
    rest_u, norm_v2, scale_v2 = data_side(1, 15, 16, squares, first_u)

    last[me_s] = jnp.broadcast_to(sum_squares(rest_u), (1, LANES))
    exchange("station", lambda peer: last.at[me_s], last.at[me_s], 17)
    out_v[...] = rbuf[1] * (scale_v2 * math.sqrt(total_cols))
    settle(17, last.at[pl.ds(0, ns - 1)])
    norm_u2 = jnp.sqrt(jnp.sum(last[...], axis=0)[:, 0:1])
    for h in range(halves):
        out_u[h : h + 1, :] = rest_u[h] * (math.sqrt(total_rows) / norm_u2)
    row = jnp.zeros((1, LANES), F32)
    row = put_lane(row, 0, norm_v1 / math.sqrt(total_cols))
    row = put_lane(row, 1, norm_u1 / math.sqrt(total_rows))
    row = put_lane(row, 2, norm_v2 / math.sqrt(total_cols))
    row = put_lane(row, 3, norm_u2 / math.sqrt(total_rows))
    out_b[...] = row

    for copy in bulk:
        copy.wait_send()
    pltpu.make_async_copy(relayed, relayed, relay_sem.at[0]).wait()
    for index, span in drains:
        pltpu.make_async_copy(span, span, send.at[index]).wait()


def solution(mesh):
    nc, ns = mesh.shape["cell"], mesh.shape["station"]

    def per_device(sensitivity, tile_mask, data_panel, model_panel):
        rows, cols = sensitivity.shape
        kd, km = data_panel.shape[0], model_panel.shape[0]
        size = kd * nc
        tiles, halves = cols // LANES, rows // LANES
        own = tiles // ns
        vmem = pl.BlockSpec(memory_space=pltpu.VMEM)
        data_vector, model_vector, bidiag = pl.pallas_call(
            functools.partial(kernel, nc, ns, rows * ns, cols * nc),
            out_shape=(
                jax.ShapeDtypeStruct((halves, LANES), F32),
                jax.ShapeDtypeStruct((tiles, LANES), F32),
                jax.ShapeDtypeStruct((1, LANES), F32),
            ),
            in_specs=[
                pl.BlockSpec(memory_space=pl.ANY),
                pl.BlockSpec(memory_space=pltpu.SMEM),
                vmem,
                pl.BlockSpec(memory_space=pl.ANY),
            ],
            out_specs=(vmem, vmem, vmem),
            scratch_shapes=[
                pltpu.VMEM((rows, cols), F32),
                pltpu.VMEM((size, tiles, LANES), F32),
                pltpu.VMEM((size, own, LANES), F32),
                pltpu.VMEM((km, cols), F32),
                pltpu.VMEM((nc, halves * kd, LANES), F32),
                pltpu.VMEM((halves, size, LANES), F32),
                pltpu.VMEM((ns, size // 4, LANES), F32),
                pltpu.VMEM((nc, size // 4, LANES), F32),
                pltpu.VMEM((ns, size // 4, LANES), F32),
                pltpu.VMEM((2, tiles, LANES), F32),
                pltpu.VMEM((2, ns, own, LANES), F32),
                pltpu.VMEM((2, tiles, LANES), F32),
                pltpu.VMEM((2, nc, 1, LANES), F32),
                pltpu.VMEM((2, ns, 1, LANES), F32),
                pltpu.VMEM((2, tiles, LANES), F32),
                pltpu.VMEM((2, nc, halves + 2, LANES), F32),
                pltpu.VMEM((2, ns, 1, LANES), F32),
                pltpu.VMEM((ns, 1, LANES), F32),
                pltpu.VMEM((rows, LANES), F32),
                pltpu.VMEM((size, LANES), F32),
                pltpu.VMEM((size, LANES), F32),
                pltpu.SemaphoreType.DMA((9,)),
                pltpu.SemaphoreType.DMA((18,)),
                pltpu.SemaphoreType.DMA((18,)),
                pltpu.SemaphoreType.DMA((ns // 2,)),
                pltpu.SemaphoreType.DMA((2,)),
                pltpu.SemaphoreType.DMA((ns // 2,)),
            ],
            compiler_params=pltpu.CompilerParams(
                collective_id=0, has_side_effects=True, vmem_limit_bytes=48 * 1024 * 1024
            ),
            name="bidiagonalise",
        )(sensitivity, tile_mask, data_panel, model_panel)
        return data_vector.reshape(rows), model_vector.reshape(cols), bidiag[0, :4]

    return jax.shard_map(
        per_device,
        mesh=mesh,
        in_specs=(P("station", "cell"), P("station", "cell"), P("cell", "station"), P("station", "cell")),
        out_specs=(P("station"), P("cell"), P()),
        check_vma=False,
    )
```

```python
import functools
import math

import jax
import jax.numpy as jnp
from jax import lax
from jax.experimental import pallas as pl
from jax.experimental.pallas import tpu as pltpu
from jax.sharding import PartitionSpec as P

TILE_ROWS = 128
TILE_COLS = 512
LANES = 128
HIGH = lax.Precision.HIGHEST
MESH = pl.DeviceIdType.MESH
F32 = jnp.float32


def eye_mask(rows):
    return lax.broadcasted_iota(jnp.int32, (rows, LANES), 0) == lax.broadcasted_iota(jnp.int32, (rows, LANES), 1)


def to_lanes(column, rows):
    return jnp.sum(jnp.where(eye_mask(rows), column, 0.0), axis=0, keepdims=True)


def to_rows(row, rows):
    return jnp.sum(jnp.where(eye_mask(rows), row, 0.0), axis=1, keepdims=True)


def lane(row, index):
    ids = lax.broadcasted_iota(jnp.int32, (1, LANES), 1)
    return jnp.sum(jnp.where(ids == index, row, 0.0), axis=1, keepdims=True)


def put_lane(row, index, value):
    ids = lax.broadcasted_iota(jnp.int32, (1, LANES), 1)
    return jnp.where(ids == index, value, row)


def total(x):
    return jnp.sum(jnp.sum(x, axis=0, keepdims=True), axis=1, keepdims=True)


def dot_t(a, b):
    return lax.dot_general(a, b, (((1,), (1,)), ((), ())), precision=HIGH, preferred_element_type=F32)


def pack(gram):
    rows = gram.shape[0] // 4
    return jnp.concatenate([gram[q * rows : (q + 1) * rows, :] for q in range(4)], axis=1)


def unpack(packed, size):
    return jnp.concatenate([packed[:, q * size : (q + 1) * size] for q in range(4)], axis=0)


def inverse(gram, size):
    rows = lax.broadcasted_iota(jnp.int32, (size, LANES), 0)
    unit = jnp.where(
        rows + size == lax.broadcasted_iota(jnp.int32, (size, LANES), 1), 1.0, 0.0
    )
    a = jnp.concatenate([gram, jnp.zeros((size, LANES - size), F32)], axis=1) + unit
    for i in range(size):
        pivot_row = a[i : i + 1, :] / a[i : i + 1, i : i + 1]
        a = jnp.where(rows == i, pivot_row, a - a[:, i : i + 1] * pivot_row)
    return jnp.concatenate([a[:, size : 2 * size], jnp.zeros((size, LANES - size), F32)], axis=1)


def kernel(
    nc, ns, total_rows, total_cols,
    sens, mask_in, dp_in, mp,
    out_u, out_v, out_b,
    g, pfull, pown, plocal, mask, dp, dloc, d1, ds, puc, pud, gu, gmc, gms,
    wpart, rs, ag, ca, rbuf, nv, fa, ubuf, ub, stack, ybuf,
    load_sem, send, recv, bulk_send, bulk_recv,
):
    me_c, me_s = lax.axis_index("cell"), lax.axis_index("station")
    nz, nx = ns // 2, min(nc, 4)
    ny = nc // nx
    me = me_c * ns + me_s
    z, core = me_s // 2, me_s % 2
    y, x = me_c // nx, me_c % nx
    rows, cols = sens.shape
    tiles = cols // LANES
    own = tiles // ns
    kd, km = dp.shape[0], mp.shape[0]
    size = kd * nc
    halves = rows // LANES
    per = TILE_COLS // LANES

    load_rows = rows // 8
    loads = [
        pltpu.make_async_copy(
            sens.at[pl.ds(q * load_rows, load_rows), :], g.at[pl.ds(q * load_rows, load_rows), :], load_sem.at[q]
        )
        for q in range(8)
    ]
    load_dp = pltpu.make_async_copy(dp_in, dp, load_sem.at[8])
    load_mp = pltpu.make_async_copy(mp, plocal, load_sem.at[9])
    load_mask = pltpu.make_async_copy(mask_in, mask, load_sem.at[10])

    def far(n):
        return sorted(range(n), key=lambda d: -min(d, n - d))

    cells = [((y + dy) % ny) * nx + (x + dx) % nx for dy in far(ny) for dx in far(nx)]
    stations = [((z + dz) % nz) * 2 + (core + dk) % 2 for dz in far(nz) for dk in (1, 0)]
    cell_peers, station_peers = cells[:-1], stations[:-1]

    barrier = pltpu.get_barrier_semaphore()
    for peer in cell_peers:
        pl.semaphore_signal(barrier, inc=1, device_id={"cell": peer}, device_id_type=MESH)
    for peer in station_peers:
        pl.semaphore_signal(barrier, inc=1, device_id={"station": peer}, device_id_type=MESH)
    for copy in [load_dp, load_mp, load_mask, *loads]:
        copy.start()

    drains = []

    def remote(src, dst, send_sem, recv_sem, where):
        return pltpu.make_async_remote_copy(
            src_ref=src, dst_ref=dst, send_sem=send_sem, recv_sem=recv_sem, device_id=where, device_id_type=MESH
        )

    def exchange(axis, src, dst, index):
        for peer in cell_peers if axis == "cell" else station_peers:
            remote(src(peer), dst, send.at[index], recv.at[index], {axis: peer}).start()

    def exchange_all(src, dst, index):
        for i, c in enumerate(cells):
            for s in stations if i < nc - 1 else station_peers:
                remote(src, dst, send.at[index], recv.at[index], {"cell": c, "station": s}).start()

    def wait_all(index, span):
        pltpu.make_async_copy(span, span, recv.at[index]).wait()
        drains.append((index, span))

    load_dp.wait()
    block = dp[...]
    for h in range(halves):
        dloc[h] = block[:, h * LANES : (h + 1) * LANES]
    d1[me_c] = dloc[...]
    ds[me_s] = dloc[...]

    load_mp.wait()

    @pl.loop(0, tiles)
    def _(j):
        piece = plocal[:, pl.ds(pl.multiple_of(j * LANES, LANES), LANES)]
        for k in range(km):
            pfull[me_s * km + k, pl.ds(j, 1), :] = piece[k : k + 1, :]

    mine = pl.ds(me_s * km, km)
    pown[mine, :, :] = pfull[mine, pl.ds(pl.multiple_of(me_s * own, own), own), :]
    pl.semaphore_wait(barrier, nc + ns - 2)

    exchange("cell", lambda peer: dloc, d1.at[me_c], 0)
    exchange("station", lambda peer: dloc, ds.at[me_s], 1)
    exchange(
        "station",
        lambda peer: pfull.at[mine, pl.ds(pl.multiple_of(peer * own, own), own), :],
        pown.at[mine, :, :],
        2,
    )
    up, down, partner = ((z + 1) % nz) * 2 + core, ((z + nz - 1) % nz) * 2 + core, z * 2 + 1 - core
    across = ((z + 2) % nz) * 2 + core
    half = tiles // 2
    bulk = {}

    def pass_on(who, at, index, target):
        view = pfull.at[pl.ds(who * km, km), at, :]
        copy = remote(view, view, bulk_send.at[index], bulk_recv.at[index], {"station": target})
        copy.start()
        bulk[index] = copy

    everything, low, high = pl.ds(0, tiles), pl.ds(0, half), pl.ds(half, half)

    def bulk_start():
        pass_on(me_s, everything, 0, up)
        pass_on(me_s, everything, 1, down)
        pass_on(me_s, everything, 2, partner)

    def bulk_relay():
        bulk[0].wait_recv()
        pass_on(down, low, 3, up)
        pass_on(down, everything, 5, partner)
        bulk[1].wait_recv()
        pass_on(up, high, 4, down)
        pass_on(up, everything, 6, partner)

    def bulk_last():
        bulk[3].wait_recv()
        pass_on(across, low, 7, partner)
        bulk[4].wait_recv()
        pass_on(across, high, 8, partner)

    def bulk_finish():
        for i in (2, 5, 6, 7, 8):
            bulk[i].wait_recv()


    wait_all(0, d1.at[pl.ds(0, nc - 1)])
    p64 = []
    for h in range(halves):
        for c in range(nc):
            pud[me_s * halves + h, c * kd : (c + 1) * kd, :] = d1[c, h]
        p64.append(pud[me_s * halves + h])
    gram = dot_t(p64[0], p64[0])
    for h in range(1, halves):
        gram = gram + dot_t(p64[h], p64[h])
    gu[me_s] = pack(gram)
    exchange("station", lambda peer: gu.at[me_s], gu.at[me_s], 3)

    wait_all(1, ds.at[pl.ds(0, ns - 1)])
    puc[:, :, me_c] = ds[...]
    exchange("cell", lambda peer: ds, puc.at[:, :, me_c], 4)

    wait_all(2, pown.at[pl.ds(0, km * (ns - 1))])
    mine_all = jnp.concatenate([pown[:, j, :] for j in range(own)], axis=1)
    gmc[me_c] = pack(dot_t(mine_all, mine_all))
    exchange("cell", lambda peer: gmc.at[me_c], gmc.at[me_c], 5)

    wait_all(3, gu.at[pl.ds(0, ns - 1)])
    bulk_start()
    t_u = inverse(unpack(jnp.sum(gu[...], axis=0), size), size)
    x_col = t_u[:, size - 1 : size] / jnp.sqrt(t_u[size - 1 : size, size - 1 : size])
    start = [jnp.sum(x_col * p64[h], axis=0, keepdims=True) for h in range(halves)]

    wait_all(5, gmc.at[pl.ds(0, nc - 1)])
    gms[me_s] = jnp.sum(gmc[...], axis=0)
    exchange("station", lambda peer: gms.at[me_s], gms.at[me_s], 6)
    load_mask.wait()
    for copy in loads:
        copy.wait()

    def adjoint(vector, t):
        for h in range(halves):
            ub[h * LANES : (h + 1) * LANES, :] = jnp.broadcast_to(to_rows(vector[h], LANES), (LANES, LANES))

        @pl.loop(0, tiles // per)
        def _(j):
            for q in range(per):
                at = pl.ds(pl.multiple_of((j * per + q) * LANES, LANES), LANES)
                result = None
                for h in range(halves):
                    parts = [None, None]
                    for r in range(h * LANES, (h + 1) * LANES, 8):
                        term = g[r : r + 8, at] * ub[r : r + 8, :]
                        w = (r // 8) % 2
                        parts[w] = term if parts[w] is None else parts[w] + term
                    part = (parts[0] + parts[1]) * mask[h, j].astype(F32)
                    result = part if result is None else result + part
                wpart[t, pl.ds(j * per + q, 1), :] = jnp.sum(result, axis=0, keepdims=True)

    def forward(t):
        def step(j, sums):
            sums = list(sums)
            for q in range(per):
                at = pl.ds(pl.multiple_of((j * per + q) * LANES, LANES), LANES)
                row = rbuf[t, pl.ds(j * per + q, 1), :]
                for h in range(halves):
                    sums[h] = sums[h] + g[h * LANES : (h + 1) * LANES, at] * (row * mask[h, j].astype(F32))
            return tuple(sums)

        sums = lax.fori_loop(0, tiles // per, step, tuple(jnp.zeros((LANES, LANES), F32) for _ in range(halves)))
        return [to_lanes(jnp.sum(part, axis=1, keepdims=True), LANES) for part in sums]

    own_at = pl.ds(pl.multiple_of(me_s * own, own), own)

    def scatter(t, index):
        rs[t, me_s] = wpart[t, own_at, :]
        exchange(
            "station",
            lambda peer: wpart.at[t, pl.ds(pl.multiple_of(peer * own, own), own), :],
            rs.at[t, me_s],
            index,
        )

    def gather(t, index_rs, index_ag):
        wait_all(index_rs, rs.at[t, pl.ds(0, ns - 1)])
        w_own = jnp.sum(rs[t], axis=0)
        ag[t, own_at, :] = w_own
        exchange("station", lambda peer: ag.at[t, own_at, :], ag.at[t, own_at, :], index_ag)
        return w_own

    def share_coef(t, coef, index):
        ca[t, me] = coef
        exchange_all(ca.at[t, me], ca.at[t, me], index)

    def summed_coef(t, index):
        wait_all(index, ca.at[t, pl.ds(0, nc * ns - 1)])
        return jnp.sum(ca[t], axis=0)

    def reorthogonalise(t, w, coef, extra, index):
        y = jnp.sum(t_m * coef, axis=1, keepdims=True)
        ybuf[...] = jnp.broadcast_to(y, (size, LANES))
        rest = w if extra is None else w - extra

        def step(k, rest):
            return rest - pfull[k] * ybuf[pl.ds(k, 1), :]

        rest = lax.fori_loop(0, size, step, rest, unroll=4)
        rbuf[t] = rest
        nv[t, me_c] = jnp.broadcast_to(total(rest * rest), (1, LANES))
        exchange("cell", lambda peer: nv.at[t, me_c], nv.at[t, me_c], index)

    def data_side(t, index_nv, index_fa, before):
        parts = forward(t)
        for h in range(halves):
            fa[t, me, h : h + 1, :] = parts[h]
        exchange_all(fa.at[t, me], fa.at[t, me], index_fa)
        wait_all(index_nv, nv.at[t, pl.ds(0, nc - 1)])
        norm_v = jnp.sqrt(jnp.sum(nv[t], axis=0)[:, 0:1])
        scale = 1.0 / norm_v
        wait_all(index_fa, fa.at[t, pl.ds(0, nc * ns - 1)])
        for s in range(ns):
            piece = fa[t, s]
            for c in range(1, nc):
                piece = piece + fa[t, c * ns + s]
            ubuf[s * halves : (s + 1) * halves, :] = piece * scale
        vec = ubuf[...]
        count = ns * halves
        col = pud[0] * vec[0:1, :]
        for i in range(1, count):
            col = col + pud[i] * vec[i : i + 1, :]
        coef = to_lanes(jnp.sum(col, axis=1, keepdims=True), size)
        y = jnp.sum(t_u * coef, axis=1, keepdims=True)
        rest = vec
        if before is not None:
            rest = rest - before * total(before * vec)
        for i in range(count):
            ubuf[i : i + 1, :] = jnp.sum(y * pud[i], axis=0, keepdims=True)
        rest = rest - ubuf[...]
        norm_u = jnp.sqrt(total(rest * rest))
        rest = rest / norm_u
        ubuf[...] = rest
        mine_u = [ubuf[pl.ds(me_s * halves + h, 1), :] for h in range(halves)]
        return rest, mine_u, norm_u, norm_v, scale

    adjoint(start, 0)
    scatter(0, 7)
    bulk_relay()
    w_own = gather(0, 7, 8)
    for k in range(size):
        stack[k : k + 1, :] = jnp.sum(pown[k] * w_own, axis=0, keepdims=True)
    share_coef(0, to_lanes(jnp.sum(stack[...], axis=1, keepdims=True), size), 9)
    wait_all(6, gms.at[pl.ds(0, ns - 1)])
    t_m = inverse(unpack(jnp.sum(gms[...], axis=0), size), size)
    bulk_last()
    wait_all(4, puc.at[:, :, pl.ds(0, nc - 1)])
    for s in range(ns):
        for h in range(halves):
            for c in range(nc):
                pud[s * halves + h, c * kd : (c + 1) * kd, :] = puc[s, h, c]
    wait_all(8, ag.at[0, pl.ds(0, own * (ns - 1)), :])
    coef = summed_coef(0, 9)
    bulk_finish()
    reorthogonalise(0, ag[0], coef, None, 10)
    first_u, mine_u, norm_u1, norm_v1, scale_v1 = data_side(0, 10, 11, None)

    adjoint(mine_u, 1)
    scatter(1, 12)
    part = wpart[1]

    def step(k, carry):
        stack[pl.ds(k, 1), :] = jnp.sum(pfull[k] * part, axis=0, keepdims=True)
        return carry

    lax.fori_loop(0, size, step, 0, unroll=4)
    coef = to_lanes(jnp.sum(stack[...], axis=1, keepdims=True), size)
    share_coef(1, put_lane(coef, size, total(rbuf[0] * part) * scale_v1), 13)
    gather(1, 12, 14)
    coef = summed_coef(1, 13)
    along = rbuf[0] * (lane(coef, size) * scale_v1)
    wait_all(14, ag.at[1, pl.ds(0, own * (ns - 1)), :])
    reorthogonalise(1, ag[1], coef, along, 15)
    second_u, mine_u, norm_u2, norm_v2, scale_v2 = data_side(1, 15, 16, first_u)

    out_v[...] = rbuf[1] * (scale_v2 * math.sqrt(total_cols))
    for h in range(halves):
        out_u[h : h + 1, :] = mine_u[h] * math.sqrt(total_rows)
    row = jnp.zeros((1, LANES), F32)
    row = put_lane(row, 0, norm_v1 / math.sqrt(total_cols))
    row = put_lane(row, 1, norm_u1 / math.sqrt(total_rows))
    row = put_lane(row, 2, norm_v2 / math.sqrt(total_cols))
    row = put_lane(row, 3, norm_u2 / math.sqrt(total_rows))
    out_b[...] = row

    for copy in bulk.values():
        copy.wait_send()
    for index, span in drains:
        pltpu.make_async_copy(span, span, send.at[index]).wait()


def solution(mesh):
    nc, ns = mesh.shape["cell"], mesh.shape["station"]

    def per_device(sensitivity, tile_mask, data_panel, model_panel):
        rows, cols = sensitivity.shape
        kd, km = data_panel.shape[0], model_panel.shape[0]
        size = kd * nc
        tiles, halves = cols // LANES, rows // LANES
        own = tiles // ns
        vmem = pl.BlockSpec(memory_space=pltpu.VMEM)
        data_vector, model_vector, bidiag = pl.pallas_call(
            functools.partial(kernel, nc, ns, rows * ns, cols * nc),
            out_shape=(
                jax.ShapeDtypeStruct((halves, LANES), F32),
                jax.ShapeDtypeStruct((tiles, LANES), F32),
                jax.ShapeDtypeStruct((1, LANES), F32),
            ),
            in_specs=[pl.BlockSpec(memory_space=pltpu.HBM)] * 4,
            out_specs=(vmem, vmem, vmem),
            scratch_shapes=[
                pltpu.VMEM((rows, cols), F32),
                pltpu.VMEM((size, tiles, LANES), F32),
                pltpu.VMEM((size, own, LANES), F32),
                pltpu.VMEM((km, cols), F32),
                pltpu.SMEM(tile_mask.shape, jnp.int32),
                pltpu.VMEM(data_panel.shape, F32),
                pltpu.VMEM((halves, kd, LANES), F32),
                pltpu.VMEM((nc, halves, kd, LANES), F32),
                pltpu.VMEM((ns, halves, kd, LANES), F32),
                pltpu.VMEM((ns, halves, nc, kd, LANES), F32),
                pltpu.VMEM((ns * halves, size, LANES), F32),
                pltpu.VMEM((ns, size // 4, LANES), F32),
                pltpu.VMEM((nc, size // 4, LANES), F32),
                pltpu.VMEM((ns, size // 4, LANES), F32),
                pltpu.VMEM((2, tiles, LANES), F32),
                pltpu.VMEM((2, ns, own, LANES), F32),
                pltpu.VMEM((2, tiles, LANES), F32),
                pltpu.VMEM((2, nc * ns, 1, LANES), F32),
                pltpu.VMEM((2, tiles, LANES), F32),
                pltpu.VMEM((2, nc, 1, LANES), F32),
                pltpu.VMEM((2, nc * ns, halves, LANES), F32),
                pltpu.VMEM((ns * halves, LANES), F32),
                pltpu.VMEM((rows, LANES), F32),
                pltpu.VMEM((size, LANES), F32),
                pltpu.VMEM((size, LANES), F32),
                pltpu.SemaphoreType.DMA((11,)),
                pltpu.SemaphoreType.DMA((17,)),
                pltpu.SemaphoreType.DMA((17,)),
                pltpu.SemaphoreType.DMA((9,)),
                pltpu.SemaphoreType.DMA((9,)),
            ],
            compiler_params=pltpu.CompilerParams(
                collective_id=0, has_side_effects=True, vmem_limit_bytes=48 * 1024 * 1024
            ),
            name="bidiagonalise",
        )(sensitivity, tile_mask, data_panel, model_panel)
        return data_vector.reshape(rows), model_vector.reshape(cols), bidiag[0, :4]

    return jax.shard_map(
        per_device,
        mesh=mesh,
        in_specs=(P("station", "cell"), P("station", "cell"), P("cell", "station"), P("station", "cell")),
        out_specs=(P("station"), P("cell"), P()),
        check_vma=False,
    )
```

```python
import functools
import math

import jax
import jax.numpy as jnp
from jax import lax
from jax.experimental import pallas as pl
from jax.experimental.pallas import tpu as pltpu
from jax.sharding import PartitionSpec as P

TILE_ROWS = 128
TILE_COLS = 512
LANES = 128
HIGH = lax.Precision.HIGHEST
MESH = pl.DeviceIdType.MESH
F32 = jnp.float32


def eye_mask(rows):
    return lax.broadcasted_iota(jnp.int32, (rows, LANES), 0) == lax.broadcasted_iota(jnp.int32, (rows, LANES), 1)


def to_lanes(column, rows):
    return jnp.sum(jnp.where(eye_mask(rows), column, 0.0), axis=0, keepdims=True)


def to_rows(row, rows):
    return jnp.sum(jnp.where(eye_mask(rows), row, 0.0), axis=1, keepdims=True)


def lane(row, index):
    ids = lax.broadcasted_iota(jnp.int32, (1, LANES), 1)
    return jnp.sum(jnp.where(ids == index, row, 0.0), axis=1, keepdims=True)


def put_lane(row, index, value):
    ids = lax.broadcasted_iota(jnp.int32, (1, LANES), 1)
    return jnp.where(ids == index, value, row)


def total(x):
    return jnp.sum(jnp.sum(x, axis=0, keepdims=True), axis=1, keepdims=True)


def dot_t(a, b):
    return lax.dot_general(a, b, (((1,), (1,)), ((), ())), precision=HIGH, preferred_element_type=F32)


def pack(gram):
    rows = gram.shape[0] // 4
    return jnp.concatenate([gram[q * rows : (q + 1) * rows, :] for q in range(4)], axis=1)


def unpack(packed, size):
    return jnp.concatenate([packed[:, q * size : (q + 1) * size] for q in range(4)], axis=0)


def inverse(gram, size):
    rows = lax.broadcasted_iota(jnp.int32, (size, LANES), 0)
    unit = jnp.where(
        rows + size == lax.broadcasted_iota(jnp.int32, (size, LANES), 1), 1.0, 0.0
    )
    a = jnp.concatenate([gram, jnp.zeros((size, LANES - size), F32)], axis=1) + unit
    for i in range(0, size, 2):
        r0, r1 = a[i : i + 1, :], a[i + 1 : i + 2, :]
        p, q, r = r0[:, i : i + 1], r0[:, i + 1 : i + 2], r1[:, i + 1 : i + 2]
        scale = 1.0 / (p * r - q * q)
        new0, new1 = (r * scale) * r0 - (q * scale) * r1, (p * scale) * r1 - (q * scale) * r0
        rest = a - a[:, i : i + 1] * new0 - a[:, i + 1 : i + 2] * new1
        a = jnp.where(rows == i, new0, jnp.where(rows == i + 1, new1, rest))
    return jnp.concatenate([a[:, size : 2 * size], jnp.zeros((size, LANES - size), F32)], axis=1)


def kernel(
    nc, ns, total_rows, total_cols,
    sens, mask_in, dp_in, mp,
    out_u, out_v, out_b,
    g, pfull, pown, plocal, mask, dp, dloc, d1, ds, puc, pud, gu, gmc, gms,
    wpart, rs, ag, ca, rbuf, nv, fa, ubuf, ub, stack, parts, ybuf,
    load_sem, send, recv, bulk_send, bulk_recv,
):
    me_c, me_s = lax.axis_index("cell"), lax.axis_index("station")
    nz, nx = ns // 2, min(nc, 4)
    ny = nc // nx
    me = me_c * ns + me_s
    z, core = me_s // 2, me_s % 2
    y, x = me_c // nx, me_c % nx
    rows, cols = sens.shape
    tiles = cols // LANES
    own = tiles // ns
    kd, km = dp.shape[0], mp.shape[0]
    size = kd * nc
    halves = rows // LANES
    per = TILE_COLS // LANES

    width = cols // ns
    loads = [
        pltpu.make_async_copy(sens.at[:, pl.ds(q * width, width)], g.at[q], load_sem.at[q]) for q in range(ns)
    ]
    load_dp = pltpu.make_async_copy(dp_in, dp, load_sem.at[ns])
    load_mp = pltpu.make_async_copy(mp, plocal, load_sem.at[ns + 1])
    load_mask = pltpu.make_async_copy(mask_in, mask, load_sem.at[ns + 2])

    def far(n):
        return sorted(range(n), key=lambda d: -min(d, n - d))

    cells = [((y + dy) % ny) * nx + (x + dx) % nx for dy in far(ny) for dx in far(nx)]
    stations = [((z + dz) % nz) * 2 + (core + dk) % 2 for dz in far(nz) for dk in (1, 0)]
    cell_peers, station_peers = cells[:-1], stations[:-1]

    barrier = pltpu.get_barrier_semaphore()
    for peer in cell_peers:
        pl.semaphore_signal(barrier, inc=1, device_id={"cell": peer}, device_id_type=MESH)
    for peer in station_peers:
        pl.semaphore_signal(barrier, inc=1, device_id={"station": peer}, device_id_type=MESH)
    for copy in [load_dp, load_mp, load_mask, *loads]:
        copy.start()

    drains = []

    def remote(src, dst, send_sem, recv_sem, where):
        return pltpu.make_async_remote_copy(
            src_ref=src, dst_ref=dst, send_sem=send_sem, recv_sem=recv_sem, device_id=where, device_id_type=MESH
        )

    def exchange(axis, src, dst, index):
        for peer in cell_peers if axis == "cell" else station_peers:
            remote(src(peer), dst, send.at[index], recv.at[index], {axis: peer}).start()

    def exchange_all(src, dst, index):
        for i, c in enumerate(cells):
            for s in stations if i < nc - 1 else station_peers:
                remote(src, dst, send.at[index], recv.at[index], {"cell": c, "station": s}).start()

    def wait_all(index, span):
        pltpu.make_async_copy(span, span, recv.at[index]).wait()
        drains.append((index, span))

    load_dp.wait()
    block = dp[...]
    for h in range(halves):
        dloc[h] = block[:, h * LANES : (h + 1) * LANES]
    d1[me_c] = dloc[...]
    ds[me_s] = dloc[...]

    load_mp.wait()

    @pl.loop(0, tiles)
    def _(j):
        piece = plocal[:, pl.ds(pl.multiple_of(j * LANES, LANES), LANES)]
        for k in range(km):
            pfull[me_s * km + k, pl.ds(j, 1), :] = piece[k : k + 1, :]

    mine = pl.ds(me_s * km, km)
    pown[mine, :, :] = pfull[mine, pl.ds(pl.multiple_of(me_s * own, own), own), :]
    pl.semaphore_wait(barrier, nc + ns - 2)

    exchange("cell", lambda peer: dloc, d1.at[me_c], 0)
    exchange("station", lambda peer: dloc, ds.at[me_s], 1)
    exchange(
        "station",
        lambda peer: pfull.at[mine, pl.ds(pl.multiple_of(peer * own, own), own), :],
        pown.at[mine, :, :],
        2,
    )
    up, down, partner = ((z + 1) % nz) * 2 + core, ((z + nz - 1) % nz) * 2 + core, z * 2 + 1 - core
    across = ((z + 2) % nz) * 2 + core
    half = tiles // 2
    bulk = {}

    def pass_on(who, at, index, target):
        view = pfull.at[pl.ds(who * km, km), at, :]
        copy = remote(view, view, bulk_send.at[index], bulk_recv.at[index], {"station": target})
        copy.start()
        bulk[index] = copy

    everything, low, high = pl.ds(0, tiles), pl.ds(0, half), pl.ds(half, half)

    def bulk_start():
        pass_on(me_s, everything, 0, up)
        pass_on(me_s, everything, 1, down)
        pass_on(me_s, everything, 2, partner)

    def bulk_relay():
        bulk[0].wait_recv()
        pass_on(down, low, 3, up)
        pass_on(down, everything, 5, partner)
        bulk[1].wait_recv()
        pass_on(up, high, 4, down)
        pass_on(up, everything, 6, partner)

    def bulk_last():
        bulk[3].wait_recv()
        pass_on(across, low, 7, partner)
        bulk[4].wait_recv()
        pass_on(across, high, 8, partner)

    def bulk_finish():
        for i in (2, 5, 6, 7, 8):
            bulk[i].wait_recv()


    wait_all(0, d1.at[pl.ds(0, nc - 1)])
    p64 = []
    for h in range(halves):
        for c in range(nc):
            pud[me_s * halves + h, c * kd : (c + 1) * kd, :] = d1[c, h]
        p64.append(pud[me_s * halves + h])
    gram = dot_t(p64[0], p64[0])
    for h in range(1, halves):
        gram = gram + dot_t(p64[h], p64[h])
    gu[me_s] = pack(gram)
    exchange("station", lambda peer: gu.at[me_s], gu.at[me_s], 3)
    bulk_start()

    wait_all(1, ds.at[pl.ds(0, ns - 1)])
    puc[:, :, me_c] = ds[...]
    exchange("cell", lambda peer: ds, puc.at[:, :, me_c], 4)

    wait_all(2, pown.at[pl.ds(0, km * (ns - 1))])
    mine_all = jnp.concatenate([pown[:, j, :] for j in range(own)], axis=1)
    gmc[me_c] = pack(dot_t(mine_all, mine_all))
    exchange("cell", lambda peer: gmc.at[me_c], gmc.at[me_c], 5)

    wait_all(3, gu.at[pl.ds(0, ns - 1)])
    t_u = inverse(unpack(jnp.sum(gu[...], axis=0), size), size)
    x_col = t_u[:, size - 1 : size] / jnp.sqrt(t_u[size - 1 : size, size - 1 : size])
    start = [jnp.sum(x_col * p64[h], axis=0, keepdims=True) for h in range(halves)]

    wait_all(5, gmc.at[pl.ds(0, nc - 1)])
    gms[me_s] = jnp.sum(gmc[...], axis=0)
    exchange("station", lambda peer: gms.at[me_s], gms.at[me_s], 6)
    load_mask.wait()
    for copy in loads:
        copy.wait()

    def adjoint(vector, t, index):
        for h in range(halves):
            ub[h * LANES : (h + 1) * LANES, :] = jnp.broadcast_to(to_rows(vector[h], LANES), (LANES, LANES))
        for s in stations:
            for h in range(halves):
                u = ub[h * LANES : (h + 1) * LANES, :]
                for i in range(own):
                    product = g[s, h * LANES : (h + 1) * LANES, i * LANES : (i + 1) * LANES] * u
                    part = jnp.sum(product.reshape(LANES // 8, 8, LANES), axis=0)
                    part = part * mask[h, s * (own // per) + i // per].astype(F32)
                    if h > 0:
                        part = part + parts[i]
                    if h < halves - 1:
                        parts[i] = part
                    else:
                        wpart[t, pl.ds(s * own + i, 1), :] = jnp.sum(part, axis=0, keepdims=True)
            there = pl.ds(pl.multiple_of(s * own, own), own)
            if s is stations[-1]:
                rs[t, me_s] = wpart[t, there, :]
            else:
                remote(wpart.at[t, there, :], rs.at[t, me_s], send.at[index], recv.at[index], {"station": s}).start()

    def forward(t):
        result = []
        for h in range(halves):

            def step(s, total_h):
                for i in range(own):
                    row = rbuf[t, pl.ds(s * own + i, 1), :] * mask[h, s * (own // per) + i // per].astype(F32)
                    total_h = total_h + g[s, h * LANES : (h + 1) * LANES, i * LANES : (i + 1) * LANES] * row
                return total_h

            total_h = lax.fori_loop(0, ns, step, jnp.zeros((LANES, LANES), F32))
            result.append(to_lanes(jnp.sum(total_h, axis=1, keepdims=True), LANES))
        return result

    own_at = pl.ds(pl.multiple_of(me_s * own, own), own)

    def panel_coef(panel, vector):
        for k in range(size):
            product = panel[k] * vector
            stack[k] = jnp.sum(product.reshape(product.shape[0] // 8, 8, LANES), axis=0)
        return to_lanes(jnp.sum(jnp.sum(stack[...], axis=1), axis=1, keepdims=True), size)

    def gather(t, index_rs, index_ag):
        wait_all(index_rs, rs.at[t, pl.ds(0, ns - 1)])
        w_own = jnp.sum(rs[t], axis=0)
        ag[t, own_at, :] = w_own
        exchange("station", lambda peer: ag.at[t, own_at, :], ag.at[t, own_at, :], index_ag)
        return w_own

    def share_coef(t, coef, index):
        ca[t, me] = coef
        exchange_all(ca.at[t, me], ca.at[t, me], index)

    def summed_coef(t, index):
        wait_all(index, ca.at[t, pl.ds(0, nc * ns - 1)])
        return jnp.sum(ca[t], axis=0)

    def reorthogonalise(t, w, coef, extra, index):
        y = jnp.sum(t_m * coef, axis=1, keepdims=True)
        ybuf[...] = jnp.broadcast_to(y, (size, LANES))
        rest = w if extra is None else w - extra
        for k in range(size):
            rest = rest - pfull[k] * ybuf[k : k + 1, :]
        rbuf[t] = rest
        nv[t, me_c] = jnp.broadcast_to(total(rest * rest), (1, LANES))
        exchange("cell", lambda peer: nv.at[t, me_c], nv.at[t, me_c], index)

    def data_side(t, index_nv, index_fa, before):
        parts = forward(t)
        for h in range(halves):
            fa[t, me, h : h + 1, :] = parts[h]
        exchange_all(fa.at[t, me], fa.at[t, me], index_fa)
        wait_all(index_nv, nv.at[t, pl.ds(0, nc - 1)])
        norm_v = jnp.sqrt(jnp.sum(nv[t], axis=0)[:, 0:1])
        scale = 1.0 / norm_v
        wait_all(index_fa, fa.at[t, pl.ds(0, nc * ns - 1)])
        for s in range(ns):
            piece = fa[t, s]
            for c in range(1, nc):
                piece = piece + fa[t, c * ns + s]
            ubuf[s * halves : (s + 1) * halves, :] = piece * scale
        vec = ubuf[...]
        count = ns * halves
        col = pud[0] * vec[0:1, :]
        for i in range(1, count):
            col = col + pud[i] * vec[i : i + 1, :]
        coef = to_lanes(jnp.sum(col, axis=1, keepdims=True), size)
        y = jnp.sum(t_u * coef, axis=1, keepdims=True)
        rest = vec
        if before is not None:
            rest = rest - before * total(before * vec)
        for i in range(count):
            ubuf[i : i + 1, :] = jnp.sum(y * pud[i], axis=0, keepdims=True)
        rest = rest - ubuf[...]
        norm_u = jnp.sqrt(total(rest * rest))
        rest = rest / norm_u
        ubuf[...] = rest
        mine_u = [ubuf[pl.ds(me_s * halves + h, 1), :] for h in range(halves)]
        return rest, mine_u, norm_u, norm_v, scale

    adjoint(start, 0, 7)
    bulk_relay()
    w_own = gather(0, 7, 8)
    share_coef(0, panel_coef(pown, w_own), 9)
    wait_all(6, gms.at[pl.ds(0, ns - 1)])
    t_m = inverse(unpack(jnp.sum(gms[...], axis=0), size), size)
    bulk_last()
    wait_all(4, puc.at[:, :, pl.ds(0, nc - 1)])
    for s in range(ns):
        for h in range(halves):
            for c in range(nc):
                pud[s * halves + h, c * kd : (c + 1) * kd, :] = puc[s, h, c]
    wait_all(8, ag.at[0, pl.ds(0, own * (ns - 1)), :])
    coef = summed_coef(0, 9)
    bulk_finish()
    reorthogonalise(0, ag[0], coef, None, 10)
    first_u, mine_u, norm_u1, norm_v1, scale_v1 = data_side(0, 10, 11, None)

    adjoint(mine_u, 1, 12)
    part = wpart[1]
    coef = panel_coef(pfull, part)
    share_coef(1, put_lane(coef, size, total(rbuf[0] * part) * scale_v1), 13)
    gather(1, 12, 14)
    coef = summed_coef(1, 13)
    along = rbuf[0] * (lane(coef, size) * scale_v1)
    wait_all(14, ag.at[1, pl.ds(0, own * (ns - 1)), :])
    reorthogonalise(1, ag[1], coef, along, 15)
    second_u, mine_u, norm_u2, norm_v2, scale_v2 = data_side(1, 15, 16, first_u)

    out_v[...] = rbuf[1] * (scale_v2 * math.sqrt(total_cols))
    for h in range(halves):
        out_u[h : h + 1, :] = mine_u[h] * math.sqrt(total_rows)
    row = jnp.zeros((1, LANES), F32)
    row = put_lane(row, 0, norm_v1 / math.sqrt(total_cols))
    row = put_lane(row, 1, norm_u1 / math.sqrt(total_rows))
    row = put_lane(row, 2, norm_v2 / math.sqrt(total_cols))
    row = put_lane(row, 3, norm_u2 / math.sqrt(total_rows))
    out_b[...] = row

    for copy in bulk.values():
        copy.wait_send()
    for index, span in drains:
        pltpu.make_async_copy(span, span, send.at[index]).wait()


def solution(mesh):
    nc, ns = mesh.shape["cell"], mesh.shape["station"]

    def per_device(sensitivity, tile_mask, data_panel, model_panel):
        rows, cols = sensitivity.shape
        kd, km = data_panel.shape[0], model_panel.shape[0]
        size = kd * nc
        tiles, halves = cols // LANES, rows // LANES
        own = tiles // ns
        vmem = pl.BlockSpec(memory_space=pltpu.VMEM)
        data_vector, model_vector, bidiag = pl.pallas_call(
            functools.partial(kernel, nc, ns, rows * ns, cols * nc),
            out_shape=(
                jax.ShapeDtypeStruct((halves, LANES), F32),
                jax.ShapeDtypeStruct((tiles, LANES), F32),
                jax.ShapeDtypeStruct((1, LANES), F32),
            ),
            in_specs=[pl.BlockSpec(memory_space=pltpu.HBM)] * 4,
            out_specs=(vmem, vmem, vmem),
            scratch_shapes=[
                pltpu.VMEM((ns, rows, cols // ns), F32),
                pltpu.VMEM((size, tiles, LANES), F32),
                pltpu.VMEM((size, own, LANES), F32),
                pltpu.VMEM((km, cols), F32),
                pltpu.SMEM(tile_mask.shape, jnp.int32),
                pltpu.VMEM(data_panel.shape, F32),
                pltpu.VMEM((halves, kd, LANES), F32),
                pltpu.VMEM((nc, halves, kd, LANES), F32),
                pltpu.VMEM((ns, halves, kd, LANES), F32),
                pltpu.VMEM((ns, halves, nc, kd, LANES), F32),
                pltpu.VMEM((ns * halves, size, LANES), F32),
                pltpu.VMEM((ns, size // 4, LANES), F32),
                pltpu.VMEM((nc, size // 4, LANES), F32),
                pltpu.VMEM((ns, size // 4, LANES), F32),
                pltpu.VMEM((2, tiles, LANES), F32),
                pltpu.VMEM((2, ns, own, LANES), F32),
                pltpu.VMEM((2, tiles, LANES), F32),
                pltpu.VMEM((2, nc * ns, 1, LANES), F32),
                pltpu.VMEM((2, tiles, LANES), F32),
                pltpu.VMEM((2, nc, 1, LANES), F32),
                pltpu.VMEM((2, nc * ns, halves, LANES), F32),
                pltpu.VMEM((ns * halves, LANES), F32),
                pltpu.VMEM((rows, LANES), F32),
                pltpu.VMEM((size, 8, LANES), F32),
                pltpu.VMEM((own, 8, LANES), F32),
                pltpu.VMEM((size, LANES), F32),
                pltpu.SemaphoreType.DMA((ns + 3,)),
                pltpu.SemaphoreType.DMA((17,)),
                pltpu.SemaphoreType.DMA((17,)),
                pltpu.SemaphoreType.DMA((9,)),
                pltpu.SemaphoreType.DMA((9,)),
            ],
            compiler_params=pltpu.CompilerParams(
                collective_id=0, has_side_effects=True, vmem_limit_bytes=48 * 1024 * 1024
            ),
            name="bidiagonalise",
        )(sensitivity, tile_mask, data_panel, model_panel)
        return data_vector.reshape(rows), model_vector.reshape(cols), bidiag[0, :4]

    return jax.shard_map(
        per_device,
        mesh=mesh,
        in_specs=(P("station", "cell"), P("station", "cell"), P("cell", "station"), P("station", "cell")),
        out_specs=(P("station"), P("cell"), P()),
        check_vma=False,
    )
```

```python
import functools
import math

import jax
import jax.numpy as jnp
from jax import lax
from jax.experimental import pallas as pl
from jax.experimental.pallas import tpu as pltpu
from jax.sharding import PartitionSpec as P

TILE_ROWS = 128
TILE_COLS = 512
LANES = 128
HIGH = lax.Precision.HIGHEST
MESH = pl.DeviceIdType.MESH
F32 = jnp.float32


def eye_mask(rows):
    return lax.broadcasted_iota(jnp.int32, (rows, LANES), 0) == lax.broadcasted_iota(jnp.int32, (rows, LANES), 1)


def to_lanes(column, rows):
    return jnp.sum(jnp.where(eye_mask(rows), column, 0.0), axis=0, keepdims=True)


def to_rows(row, rows):
    return jnp.sum(jnp.where(eye_mask(rows), row, 0.0), axis=1, keepdims=True)


def lane(row, index):
    ids = lax.broadcasted_iota(jnp.int32, (1, LANES), 1)
    return jnp.sum(jnp.where(ids == index, row, 0.0), axis=1, keepdims=True)


def put_lane(row, index, value):
    ids = lax.broadcasted_iota(jnp.int32, (1, LANES), 1)
    return jnp.where(ids == index, value, row)


def total(x):
    return jnp.sum(jnp.sum(x, axis=0, keepdims=True), axis=1, keepdims=True)


def dot_t(a, b):
    return lax.dot_general(a, b, (((1,), (1,)), ((), ())), precision=HIGH, preferred_element_type=F32)


def pack(gram):
    rows = gram.shape[0] // 4
    return jnp.concatenate([gram[q * rows : (q + 1) * rows, :] for q in range(4)], axis=1)


def unpack(packed, size):
    return jnp.concatenate([packed[:, q * size : (q + 1) * size] for q in range(4)], axis=0)


def inverse(gram, size):
    rows = lax.broadcasted_iota(jnp.int32, (size, LANES), 0)
    unit = jnp.where(
        rows + size == lax.broadcasted_iota(jnp.int32, (size, LANES), 1), 1.0, 0.0
    )
    a = jnp.concatenate([gram, jnp.zeros((size, LANES - size), F32)], axis=1) + unit
    for i in range(size):
        pivot_row = a[i : i + 1, :] / a[i : i + 1, i : i + 1]
        a = jnp.where(rows == i, pivot_row, a - a[:, i : i + 1] * pivot_row)
    return jnp.concatenate([a[:, size : 2 * size], jnp.zeros((size, LANES - size), F32)], axis=1)


def kernel(
    nc, ns, total_rows, total_cols,
    sens, mask_in, dp_in, mp,
    out_u, out_v, out_b,
    g, pfull, pown, plocal, mask, dp, dloc, d1, ds, puc, pud, gu, gmc, gms,
    wpart, rs, ag, ca, rbuf, nv, fa, ubuf, ub, stack, parts, ybuf,
    load_sem, send, recv, bulk_send, bulk_recv,
):
    me_c, me_s = lax.axis_index("cell"), lax.axis_index("station")
    nz, nx = ns // 2, min(nc, 4)
    ny = nc // nx
    me = me_c * ns + me_s
    z, core = me_s // 2, me_s % 2
    y, x = me_c // nx, me_c % nx
    rows, cols = sens.shape
    tiles = cols // LANES
    own = tiles // ns
    kd, km = dp.shape[0], mp.shape[0]
    size = kd * nc
    halves = rows // LANES
    per = TILE_COLS // LANES

    width = cols // ns
    loads = [
        pltpu.make_async_copy(sens.at[:, pl.ds(q * width, width)], g.at[q], load_sem.at[q]) for q in range(ns)
    ]
    load_dp = pltpu.make_async_copy(dp_in, dp, load_sem.at[ns])
    load_mp = pltpu.make_async_copy(mp, plocal, load_sem.at[ns + 1])
    load_mask = pltpu.make_async_copy(mask_in, mask, load_sem.at[ns + 2])

    def far(n):
        return sorted(range(n), key=lambda d: -min(d, n - d))

    cells = [((y + dy) % ny) * nx + (x + dx) % nx for dy in far(ny) for dx in far(nx)]
    stations = [((z + dz) % nz) * 2 + (core + dk) % 2 for dz in far(nz) for dk in (1, 0)]
    cell_peers, station_peers = cells[:-1], stations[:-1]

    barrier = pltpu.get_barrier_semaphore()
    for peer in cell_peers:
        pl.semaphore_signal(barrier, inc=1, device_id={"cell": peer}, device_id_type=MESH)
    for peer in station_peers:
        pl.semaphore_signal(barrier, inc=1, device_id={"station": peer}, device_id_type=MESH)
    for copy in [load_dp, load_mp, load_mask, *loads]:
        copy.start()

    drains = []

    def remote(src, dst, send_sem, recv_sem, where):
        return pltpu.make_async_remote_copy(
            src_ref=src, dst_ref=dst, send_sem=send_sem, recv_sem=recv_sem, device_id=where, device_id_type=MESH
        )

    def exchange(axis, src, dst, index):
        for peer in cell_peers if axis == "cell" else station_peers:
            remote(src(peer), dst, send.at[index], recv.at[index], {axis: peer}).start()

    def exchange_all(src, dst, index):
        for i, c in enumerate(cells):
            for s in stations if i < nc - 1 else station_peers:
                remote(src, dst, send.at[index], recv.at[index], {"cell": c, "station": s}).start()

    def wait_all(index, span):
        pltpu.make_async_copy(span, span, recv.at[index]).wait()
        drains.append((index, span))

    load_dp.wait()
    block = dp[...]
    for h in range(halves):
        dloc[h] = block[:, h * LANES : (h + 1) * LANES]
    d1[me_c] = dloc[...]
    ds[me_s] = dloc[...]

    load_mp.wait()

    @pl.loop(0, tiles)
    def _(j):
        piece = plocal[:, pl.ds(pl.multiple_of(j * LANES, LANES), LANES)]
        for k in range(km):
            pfull[me_s * km + k, pl.ds(j, 1), :] = piece[k : k + 1, :]

    mine = pl.ds(me_s * km, km)
    pown[mine, :, :] = pfull[mine, pl.ds(pl.multiple_of(me_s * own, own), own), :]
    pl.semaphore_wait(barrier, nc + ns - 2)

    exchange("cell", lambda peer: dloc, d1.at[me_c], 0)
    exchange("station", lambda peer: dloc, ds.at[me_s], 1)
    exchange(
        "station",
        lambda peer: pfull.at[mine, pl.ds(pl.multiple_of(peer * own, own), own), :],
        pown.at[mine, :, :],
        2,
    )
    up, down, partner = ((z + 1) % nz) * 2 + core, ((z + nz - 1) % nz) * 2 + core, z * 2 + 1 - core
    across = ((z + 2) % nz) * 2 + core
    half = tiles // 2
    bulk = {}

    def pass_on(who, at, index, target):
        view = pfull.at[pl.ds(who * km, km), at, :]
        copy = remote(view, view, bulk_send.at[index], bulk_recv.at[index], {"station": target})
        copy.start()
        bulk[index] = copy

    everything, low, high = pl.ds(0, tiles), pl.ds(0, half), pl.ds(half, half)

    def bulk_start():
        pass_on(me_s, everything, 0, up)
        pass_on(me_s, everything, 1, down)
        pass_on(me_s, everything, 2, partner)

    def bulk_relay():
        bulk[0].wait_recv()
        pass_on(down, low, 3, up)
        pass_on(down, everything, 5, partner)
        bulk[1].wait_recv()
        pass_on(up, high, 4, down)
        pass_on(up, everything, 6, partner)

    def bulk_last():
        bulk[3].wait_recv()
        pass_on(across, low, 7, partner)
        bulk[4].wait_recv()
        pass_on(across, high, 8, partner)

    def bulk_finish():
        for i in (2, 5, 6, 7, 8):
            bulk[i].wait_recv()


    wait_all(0, d1.at[pl.ds(0, nc - 1)])
    p64 = []
    for h in range(halves):
        for c in range(nc):
            pud[me_s * halves + h, c * kd : (c + 1) * kd, :] = d1[c, h]
        p64.append(pud[me_s * halves + h])
    gram = dot_t(p64[0], p64[0])
    for h in range(1, halves):
        gram = gram + dot_t(p64[h], p64[h])
    gu[me_s] = pack(gram)
    exchange("station", lambda peer: gu.at[me_s], gu.at[me_s], 3)
    bulk_start()

    wait_all(1, ds.at[pl.ds(0, ns - 1)])
    puc[:, :, me_c] = ds[...]
    exchange("cell", lambda peer: ds, puc.at[:, :, me_c], 4)

    wait_all(2, pown.at[pl.ds(0, km * (ns - 1))])
    mine_all = jnp.concatenate([pown[:, j, :] for j in range(own)], axis=1)
    gmc[me_c] = pack(dot_t(mine_all, mine_all))
    exchange("cell", lambda peer: gmc.at[me_c], gmc.at[me_c], 5)

    wait_all(3, gu.at[pl.ds(0, ns - 1)])
    t_u = inverse(unpack(jnp.sum(gu[...], axis=0), size), size)
    x_col = t_u[:, size - 1 : size] / jnp.sqrt(t_u[size - 1 : size, size - 1 : size])
    start = [jnp.sum(x_col * p64[h], axis=0, keepdims=True) for h in range(halves)]

    wait_all(5, gmc.at[pl.ds(0, nc - 1)])
    gms[me_s] = jnp.sum(gmc[...], axis=0)
    exchange("station", lambda peer: gms.at[me_s], gms.at[me_s], 6)
    load_mask.wait()
    for copy in loads:
        copy.wait()

    def adjoint(vector, t, index):
        for h in range(halves):
            ub[h * LANES : (h + 1) * LANES, :] = jnp.broadcast_to(to_rows(vector[h], LANES), (LANES, LANES))
        for s in stations:
            for h in range(halves):
                u = ub[h * LANES : (h + 1) * LANES, :]
                for i in range(own):
                    product = g[s, h * LANES : (h + 1) * LANES, i * LANES : (i + 1) * LANES] * u
                    part = jnp.sum(product.reshape(LANES // 8, 8, LANES), axis=0)
                    part = part * mask[h, s * (own // per) + i // per].astype(F32)
                    if h > 0:
                        part = part + parts[i]
                    if h < halves - 1:
                        parts[i] = part
                    else:
                        wpart[t, pl.ds(s * own + i, 1), :] = jnp.sum(part, axis=0, keepdims=True)
            there = pl.ds(pl.multiple_of(s * own, own), own)
            if s is stations[-1]:
                rs[t, me_s] = wpart[t, there, :]
            else:
                remote(wpart.at[t, there, :], rs.at[t, me_s], send.at[index], recv.at[index], {"station": s}).start()

    def forward(t):
        result = []
        for h in range(halves):

            def step(s, total_h):
                for i in range(own):
                    row = rbuf[t, pl.ds(s * own + i, 1), :] * mask[h, s * (own // per) + i // per].astype(F32)
                    total_h = total_h + g[s, h * LANES : (h + 1) * LANES, i * LANES : (i + 1) * LANES] * row
                return total_h

            total_h = lax.fori_loop(0, ns, step, jnp.zeros((LANES, LANES), F32))
            result.append(to_lanes(jnp.sum(total_h, axis=1, keepdims=True), LANES))
        return result

    own_at = pl.ds(pl.multiple_of(me_s * own, own), own)

    def panel_coef(panel, vector):
        for k in range(size):
            product = panel[k] * vector
            stack[k] = jnp.sum(product.reshape(product.shape[0] // 8, 8, LANES), axis=0)
        return to_lanes(jnp.sum(jnp.sum(stack[...], axis=1), axis=1, keepdims=True), size)

    def gather(t, index_rs, index_ag):
        wait_all(index_rs, rs.at[t, pl.ds(0, ns - 1)])
        w_own = jnp.sum(rs[t], axis=0)
        ag[t, own_at, :] = w_own
        exchange("station", lambda peer: ag.at[t, own_at, :], ag.at[t, own_at, :], index_ag)
        return w_own

    def share_coef(t, coef, index):
        ca[t, me] = coef
        exchange_all(ca.at[t, me], ca.at[t, me], index)

    def summed_coef(t, index):
        wait_all(index, ca.at[t, pl.ds(0, nc * ns - 1)])
        return jnp.sum(ca[t], axis=0)

    def reorthogonalise(t, w, coef, extra, index):
        y = jnp.sum(t_m * coef, axis=1, keepdims=True)
        ybuf[...] = jnp.broadcast_to(y, (size, LANES))
        rest = w if extra is None else w - extra
        for k in range(size):
            rest = rest - pfull[k] * ybuf[k : k + 1, :]
        rbuf[t] = rest
        nv[t, me_c] = jnp.broadcast_to(total(rest * rest), (1, LANES))
        exchange("cell", lambda peer: nv.at[t, me_c], nv.at[t, me_c], index)

    def data_side(t, index_nv, index_fa, before):
        parts = forward(t)
        for h in range(halves):
            fa[t, me, h : h + 1, :] = parts[h]
        exchange_all(fa.at[t, me], fa.at[t, me], index_fa)
        wait_all(index_nv, nv.at[t, pl.ds(0, nc - 1)])
        norm_v = jnp.sqrt(jnp.sum(nv[t], axis=0)[:, 0:1])
        scale = 1.0 / norm_v
        wait_all(index_fa, fa.at[t, pl.ds(0, nc * ns - 1)])
        for s in range(ns):
            piece = fa[t, s]
            for c in range(1, nc):
                piece = piece + fa[t, c * ns + s]
            ubuf[s * halves : (s + 1) * halves, :] = piece * scale
        vec = ubuf[...]
        count = ns * halves
        col = pud[0] * vec[0:1, :]
        for i in range(1, count):
            col = col + pud[i] * vec[i : i + 1, :]
        coef = to_lanes(jnp.sum(col, axis=1, keepdims=True), size)
        y = jnp.sum(t_u * coef, axis=1, keepdims=True)
        rest = vec
        if before is not None:
            rest = rest - before * total(before * vec)
        for i in range(count):
            ubuf[i : i + 1, :] = jnp.sum(y * pud[i], axis=0, keepdims=True)
        rest = rest - ubuf[...]
        norm_u = jnp.sqrt(total(rest * rest))
        rest = rest / norm_u
        ubuf[...] = rest
        mine_u = [ubuf[pl.ds(me_s * halves + h, 1), :] for h in range(halves)]
        return rest, mine_u, norm_u, norm_v, scale

    adjoint(start, 0, 7)
    bulk_relay()
    w_own = gather(0, 7, 8)
    share_coef(0, panel_coef(pown, w_own), 9)
    wait_all(6, gms.at[pl.ds(0, ns - 1)])
    t_m = inverse(unpack(jnp.sum(gms[...], axis=0), size), size)
    bulk_last()
    wait_all(4, puc.at[:, :, pl.ds(0, nc - 1)])
    for s in range(ns):
        for h in range(halves):
            for c in range(nc):
                pud[s * halves + h, c * kd : (c + 1) * kd, :] = puc[s, h, c]
    wait_all(8, ag.at[0, pl.ds(0, own * (ns - 1)), :])
    coef = summed_coef(0, 9)
    bulk_finish()
    reorthogonalise(0, ag[0], coef, None, 10)
    first_u, mine_u, norm_u1, norm_v1, scale_v1 = data_side(0, 10, 11, None)

    adjoint(mine_u, 1, 12)
    part = wpart[1]
    coef = panel_coef(pfull, part)
    share_coef(1, put_lane(coef, size, total(rbuf[0] * part) * scale_v1), 13)
    gather(1, 12, 14)
    coef = summed_coef(1, 13)
    along = rbuf[0] * (lane(coef, size) * scale_v1)
    wait_all(14, ag.at[1, pl.ds(0, own * (ns - 1)), :])
    reorthogonalise(1, ag[1], coef, along, 15)
    second_u, mine_u, norm_u2, norm_v2, scale_v2 = data_side(1, 15, 16, first_u)

    out_v[...] = rbuf[1] * (scale_v2 * math.sqrt(total_cols))
    for h in range(halves):
        out_u[h : h + 1, :] = mine_u[h] * math.sqrt(total_rows)
    row = jnp.zeros((1, LANES), F32)
    row = put_lane(row, 0, norm_v1 / math.sqrt(total_cols))
    row = put_lane(row, 1, norm_u1 / math.sqrt(total_rows))
    row = put_lane(row, 2, norm_v2 / math.sqrt(total_cols))
    row = put_lane(row, 3, norm_u2 / math.sqrt(total_rows))
    out_b[...] = row

    for copy in bulk.values():
        copy.wait_send()
    for index, span in drains:
        pltpu.make_async_copy(span, span, send.at[index]).wait()


def solution(mesh):
    nc, ns = mesh.shape["cell"], mesh.shape["station"]

    def per_device(sensitivity, tile_mask, data_panel, model_panel):
        rows, cols = sensitivity.shape
        kd, km = data_panel.shape[0], model_panel.shape[0]
        size = kd * nc
        tiles, halves = cols // LANES, rows // LANES
        own = tiles // ns
        vmem = pl.BlockSpec(memory_space=pltpu.VMEM)
        data_vector, model_vector, bidiag = pl.pallas_call(
            functools.partial(kernel, nc, ns, rows * ns, cols * nc),
            out_shape=(
                jax.ShapeDtypeStruct((halves, LANES), F32),
                jax.ShapeDtypeStruct((tiles, LANES), F32),
                jax.ShapeDtypeStruct((1, LANES), F32),
            ),
            in_specs=[pl.BlockSpec(memory_space=pltpu.HBM)] * 4,
            out_specs=(vmem, vmem, vmem),
            scratch_shapes=[
                pltpu.VMEM((ns, rows, cols // ns), F32),
                pltpu.VMEM((size, tiles, LANES), F32),
                pltpu.VMEM((size, own, LANES), F32),
                pltpu.VMEM((km, cols), F32),
                pltpu.SMEM(tile_mask.shape, jnp.int32),
                pltpu.VMEM(data_panel.shape, F32),
                pltpu.VMEM((halves, kd, LANES), F32),
                pltpu.VMEM((nc, halves, kd, LANES), F32),
                pltpu.VMEM((ns, halves, kd, LANES), F32),
                pltpu.VMEM((ns, halves, nc, kd, LANES), F32),
                pltpu.VMEM((ns * halves, size, LANES), F32),
                pltpu.VMEM((ns, size // 4, LANES), F32),
                pltpu.VMEM((nc, size // 4, LANES), F32),
                pltpu.VMEM((ns, size // 4, LANES), F32),
                pltpu.VMEM((2, tiles, LANES), F32),
                pltpu.VMEM((2, ns, own, LANES), F32),
                pltpu.VMEM((2, tiles, LANES), F32),
                pltpu.VMEM((2, nc * ns, 1, LANES), F32),
                pltpu.VMEM((2, tiles, LANES), F32),
                pltpu.VMEM((2, nc, 1, LANES), F32),
                pltpu.VMEM((2, nc * ns, halves, LANES), F32),
                pltpu.VMEM((ns * halves, LANES), F32),
                pltpu.VMEM((rows, LANES), F32),
                pltpu.VMEM((size, 8, LANES), F32),
                pltpu.VMEM((own, 8, LANES), F32),
                pltpu.VMEM((size, LANES), F32),
                pltpu.SemaphoreType.DMA((ns + 3,)),
                pltpu.SemaphoreType.DMA((17,)),
                pltpu.SemaphoreType.DMA((17,)),
                pltpu.SemaphoreType.DMA((9,)),
                pltpu.SemaphoreType.DMA((9,)),
            ],
            compiler_params=pltpu.CompilerParams(
                collective_id=0, has_side_effects=True, vmem_limit_bytes=48 * 1024 * 1024
            ),
            name="bidiagonalise",
        )(sensitivity, tile_mask, data_panel, model_panel)
        return data_vector.reshape(rows), model_vector.reshape(cols), bidiag[0, :4]

    return jax.shard_map(
        per_device,
        mesh=mesh,
        in_specs=(P("station", "cell"), P("station", "cell"), P("cell", "station"), P("station", "cell")),
        out_specs=(P("station"), P("cell"), P()),
        check_vma=False,
    )
```

```python
import functools
import math

import jax
import jax.numpy as jnp
from jax import lax
from jax.experimental import pallas as pl
from jax.experimental.pallas import tpu as pltpu
from jax.sharding import PartitionSpec as P

TILE_ROWS = 128
TILE_COLS = 512
LANES = 128
HIGH = lax.Precision.HIGHEST
MESH = pl.DeviceIdType.MESH
F32 = jnp.float32


def eye_mask(rows):
    return lax.broadcasted_iota(jnp.int32, (rows, LANES), 0) == lax.broadcasted_iota(jnp.int32, (rows, LANES), 1)


def to_lanes(column, rows):
    return jnp.sum(jnp.where(eye_mask(rows), column, 0.0), axis=0, keepdims=True)


def to_rows(row, rows):
    return jnp.sum(jnp.where(eye_mask(rows), row, 0.0), axis=1, keepdims=True)


def lane(row, index):
    ids = lax.broadcasted_iota(jnp.int32, (1, LANES), 1)
    return jnp.sum(jnp.where(ids == index, row, 0.0), axis=1, keepdims=True)


def put_lane(row, index, value):
    ids = lax.broadcasted_iota(jnp.int32, (1, LANES), 1)
    return jnp.where(ids == index, value, row)


def total(x):
    return jnp.sum(jnp.sum(x, axis=0, keepdims=True), axis=1, keepdims=True)


def dot_t(a, b):
    return lax.dot_general(a, b, (((1,), (1,)), ((), ())), precision=HIGH, preferred_element_type=F32)


def pack(gram):
    rows = gram.shape[0] // 4
    return jnp.concatenate([gram[q * rows : (q + 1) * rows, :] for q in range(4)], axis=1)


def unpack(packed, size):
    return jnp.concatenate([packed[:, q * size : (q + 1) * size] for q in range(4)], axis=0)


def inverse(gram, size):
    rows = lax.broadcasted_iota(jnp.int32, (size, LANES), 0)
    unit = jnp.where(
        rows + size == lax.broadcasted_iota(jnp.int32, (size, LANES), 1), 1.0, 0.0
    )
    a = jnp.concatenate([gram, jnp.zeros((size, LANES - size), F32)], axis=1) + unit
    for i in range(size):
        pivot_row = a[i : i + 1, :] / a[i : i + 1, i : i + 1]
        a = jnp.where(rows == i, pivot_row, a - a[:, i : i + 1] * pivot_row)
    return jnp.concatenate([a[:, size : 2 * size], jnp.zeros((size, LANES - size), F32)], axis=1)


def kernel(
    nc, ns, total_rows, total_cols,
    sens, mask_in, dp_in, mp,
    out_u, out_v, out_b,
    g, pfull, pown, plocal, mask, dp, dloc, d1, ds, puc, pud, gu, gmc, gms,
    wpart, rs, ag, ca, rbuf, nv, fa, ubuf, ub, stack, parts, ybuf,
    load_sem, send, recv, bulk_send, bulk_recv,
):
    me_c, me_s = lax.axis_index("cell"), lax.axis_index("station")
    nz, nx = ns // 2, min(nc, 4)
    ny = nc // nx
    me = me_c * ns + me_s
    z, core = me_s // 2, me_s % 2
    y, x = me_c // nx, me_c % nx
    rows, cols = sens.shape
    tiles = cols // LANES
    own = tiles // ns
    kd, km = dp.shape[0], mp.shape[0]
    size = kd * nc
    halves = rows // LANES
    per = TILE_COLS // LANES

    width = cols // ns
    loads = [
        pltpu.make_async_copy(sens.at[:, pl.ds(q * width, width)], g.at[q], load_sem.at[q]) for q in range(ns)
    ]
    load_dp = pltpu.make_async_copy(dp_in, dp, load_sem.at[ns])
    load_mp = pltpu.make_async_copy(mp, plocal, load_sem.at[ns + 1])
    load_mask = pltpu.make_async_copy(mask_in, mask, load_sem.at[ns + 2])

    def far(n):
        return sorted(range(n), key=lambda d: -min(d, n - d))

    cells = [((y + dy) % ny) * nx + (x + dx) % nx for dy in far(ny) for dx in far(nx)]
    stations = [((z + dz) % nz) * 2 + (core + dk) % 2 for dz in far(nz) for dk in (1, 0)]
    cell_peers, station_peers = cells[:-1], stations[:-1]

    barrier = pltpu.get_barrier_semaphore()
    for peer in cell_peers:
        pl.semaphore_signal(barrier, inc=1, device_id={"cell": peer}, device_id_type=MESH)
    for peer in station_peers:
        pl.semaphore_signal(barrier, inc=1, device_id={"station": peer}, device_id_type=MESH)
    for copy in [load_dp, load_mp, load_mask, *loads]:
        copy.start()

    drains = []

    def remote(src, dst, send_sem, recv_sem, where):
        return pltpu.make_async_remote_copy(
            src_ref=src, dst_ref=dst, send_sem=send_sem, recv_sem=recv_sem, device_id=where, device_id_type=MESH
        )

    def exchange(axis, src, dst, index):
        for peer in cell_peers if axis == "cell" else station_peers:
            remote(src(peer), dst, send.at[index], recv.at[index], {axis: peer}).start()

    def exchange_all(src, dst, index):
        for i, c in enumerate(cells):
            for s in stations if i < nc - 1 else station_peers:
                remote(src, dst, send.at[index], recv.at[index], {"cell": c, "station": s}).start()

    def wait_all(index, span):
        pltpu.make_async_copy(span, span, recv.at[index]).wait()
        drains.append((index, span))

    load_dp.wait()
    block = dp[...]
    for h in range(halves):
        dloc[h] = block[:, h * LANES : (h + 1) * LANES]
    d1[me_c] = dloc[...]
    ds[me_s] = dloc[...]

    load_mp.wait()

    @pl.loop(0, tiles)
    def _(j):
        piece = plocal[:, pl.ds(pl.multiple_of(j * LANES, LANES), LANES)]
        for k in range(km):
            pfull[me_s * km + k, pl.ds(j, 1), :] = piece[k : k + 1, :]

    mine = pl.ds(me_s * km, km)
    pown[mine, :, :] = pfull[mine, pl.ds(pl.multiple_of(me_s * own, own), own), :]
    pl.semaphore_wait(barrier, nc + ns - 2)

    exchange("cell", lambda peer: dloc, d1.at[me_c], 0)
    exchange("station", lambda peer: dloc, ds.at[me_s], 1)
    exchange(
        "station",
        lambda peer: pfull.at[mine, pl.ds(pl.multiple_of(peer * own, own), own), :],
        pown.at[mine, :, :],
        2,
    )
    up, down, partner = ((z + 1) % nz) * 2 + core, ((z + nz - 1) % nz) * 2 + core, z * 2 + 1 - core
    across = ((z + 2) % nz) * 2 + core
    half = tiles // 2
    bulk = {}

    def pass_on(who, at, index, target):
        view = pfull.at[pl.ds(who * km, km), at, :]
        copy = remote(view, view, bulk_send.at[index], bulk_recv.at[index], {"station": target})
        copy.start()
        bulk[index] = copy

    everything, low, high = pl.ds(0, tiles), pl.ds(0, half), pl.ds(half, half)

    def bulk_start():
        pass_on(me_s, everything, 0, up)
        pass_on(me_s, everything, 1, down)
        pass_on(me_s, everything, 2, partner)

    def bulk_relay():
        bulk[0].wait_recv()
        pass_on(down, low, 3, up)
        pass_on(down, everything, 5, partner)
        bulk[1].wait_recv()
        pass_on(up, high, 4, down)
        pass_on(up, everything, 6, partner)

    def bulk_last():
        bulk[3].wait_recv()
        pass_on(across, low, 7, partner)
        bulk[4].wait_recv()
        pass_on(across, high, 8, partner)

    def bulk_finish():
        for i in (2, 5, 6, 7, 8):
            bulk[i].wait_recv()


    wait_all(0, d1.at[pl.ds(0, nc - 1)])
    p64 = []
    for h in range(halves):
        for c in range(nc):
            pud[me_s * halves + h, c * kd : (c + 1) * kd, :] = d1[c, h]
        p64.append(pud[me_s * halves + h])
    gram = dot_t(p64[0], p64[0])
    for h in range(1, halves):
        gram = gram + dot_t(p64[h], p64[h])
    gu[me_s] = pack(gram)
    exchange("station", lambda peer: gu.at[me_s], gu.at[me_s], 3)
    bulk_start()

    wait_all(1, ds.at[pl.ds(0, ns - 1)])
    puc[:, :, me_c] = ds[...]
    exchange("cell", lambda peer: ds, puc.at[:, :, me_c], 4)

    wait_all(2, pown.at[pl.ds(0, km * (ns - 1))])
    mine_all = jnp.concatenate([pown[:, j, :] for j in range(own)], axis=1)
    gmc[me_c] = pack(dot_t(mine_all, mine_all))
    exchange("cell", lambda peer: gmc.at[me_c], gmc.at[me_c], 5)

    wait_all(3, gu.at[pl.ds(0, ns - 1)])
    t_u = inverse(unpack(jnp.sum(gu[...], axis=0), size), size)
    x_col = t_u[:, size - 1 : size] / jnp.sqrt(t_u[size - 1 : size, size - 1 : size])
    start = [jnp.sum(x_col * p64[h], axis=0, keepdims=True) for h in range(halves)]

    load_mask.wait()
    for copy in loads:
        copy.wait()

    def adjoint(vector, t, index):
        for h in range(halves):
            ub[h * LANES : (h + 1) * LANES, :] = jnp.broadcast_to(to_rows(vector[h], LANES), (LANES, LANES))
        for s in stations:
            for h in range(halves):
                u = ub[h * LANES : (h + 1) * LANES, :]
                for i in range(own):
                    product = g[s, h * LANES : (h + 1) * LANES, i * LANES : (i + 1) * LANES] * u
                    part = jnp.sum(product.reshape(LANES // 8, 8, LANES), axis=0)
                    part = part * mask[h, s * (own // per) + i // per].astype(F32)
                    if h > 0:
                        part = part + parts[i]
                    if h < halves - 1:
                        parts[i] = part
                    else:
                        wpart[t, pl.ds(s * own + i, 1), :] = jnp.sum(part, axis=0, keepdims=True)
            there = pl.ds(pl.multiple_of(s * own, own), own)
            if s is stations[-1]:
                rs[t, me_s] = wpart[t, there, :]
            else:
                remote(wpart.at[t, there, :], rs.at[t, me_s], send.at[index], recv.at[index], {"station": s}).start()

    def forward(t):
        result = []
        for h in range(halves):

            def step(s, total_h):
                for i in range(own):
                    row = rbuf[t, pl.ds(s * own + i, 1), :] * mask[h, s * (own // per) + i // per].astype(F32)
                    total_h = total_h + g[s, h * LANES : (h + 1) * LANES, i * LANES : (i + 1) * LANES] * row
                return total_h

            total_h = lax.fori_loop(0, ns, step, jnp.zeros((LANES, LANES), F32))
            result.append(to_lanes(jnp.sum(total_h, axis=1, keepdims=True), LANES))
        return result

    own_at = pl.ds(pl.multiple_of(me_s * own, own), own)

    def panel_coef(panel, vector):
        for k in range(size):
            product = panel[k] * vector
            stack[k] = jnp.sum(product.reshape(product.shape[0] // 8, 8, LANES), axis=0)
        return to_lanes(jnp.sum(jnp.sum(stack[...], axis=1), axis=1, keepdims=True), size)

    def gather(t, index_rs, index_ag):
        wait_all(index_rs, rs.at[t, pl.ds(0, ns - 1)])
        w_own = jnp.sum(rs[t], axis=0)
        ag[t, own_at, :] = w_own
        exchange("station", lambda peer: ag.at[t, own_at, :], ag.at[t, own_at, :], index_ag)
        return w_own

    def share_coef(t, coef, index):
        ca[t, me] = coef
        exchange_all(ca.at[t, me], ca.at[t, me], index)

    def summed_coef(t, index):
        wait_all(index, ca.at[t, pl.ds(0, nc * ns - 1)])
        return jnp.sum(ca[t], axis=0)

    def reorthogonalise(t, w, coef, extra, index):
        y = jnp.sum(t_m * coef, axis=1, keepdims=True)
        ybuf[...] = jnp.broadcast_to(y, (size, LANES))
        rest = w if extra is None else w - extra
        for k in range(size):
            rest = rest - pfull[k] * ybuf[k : k + 1, :]
        rbuf[t] = rest
        nv[t, me_c] = jnp.broadcast_to(total(rest * rest), (1, LANES))
        exchange("cell", lambda peer: nv.at[t, me_c], nv.at[t, me_c], index)

    def data_side(t, index_nv, index_fa, before):
        parts = forward(t)
        for h in range(halves):
            fa[t, me, h : h + 1, :] = parts[h]
        exchange_all(fa.at[t, me], fa.at[t, me], index_fa)
        wait_all(index_nv, nv.at[t, pl.ds(0, nc - 1)])
        norm_v = jnp.sqrt(jnp.sum(nv[t], axis=0)[:, 0:1])
        scale = 1.0 / norm_v
        wait_all(index_fa, fa.at[t, pl.ds(0, nc * ns - 1)])
        for s in range(ns):
            piece = fa[t, s]
            for c in range(1, nc):
                piece = piece + fa[t, c * ns + s]
            ubuf[s * halves : (s + 1) * halves, :] = piece * scale
        vec = ubuf[...]
        count = ns * halves
        col = pud[0] * vec[0:1, :]
        for i in range(1, count):
            col = col + pud[i] * vec[i : i + 1, :]
        coef = to_lanes(jnp.sum(col, axis=1, keepdims=True), size)
        y = jnp.sum(t_u * coef, axis=1, keepdims=True)
        rest = vec
        if before is not None:
            rest = rest - before * total(before * vec)
        for i in range(count):
            ubuf[i : i + 1, :] = jnp.sum(y * pud[i], axis=0, keepdims=True)
        rest = rest - ubuf[...]
        norm_u = jnp.sqrt(total(rest * rest))
        rest = rest / norm_u
        ubuf[...] = rest
        mine_u = [ubuf[pl.ds(me_s * halves + h, 1), :] for h in range(halves)]
        return rest, mine_u, norm_u, norm_v, scale

    adjoint(start, 0, 7)
    wait_all(5, gmc.at[pl.ds(0, nc - 1)])
    gms[me_s] = jnp.sum(gmc[...], axis=0)
    exchange("station", lambda peer: gms.at[me_s], gms.at[me_s], 6)
    bulk_relay()
    w_own = gather(0, 7, 8)
    share_coef(0, panel_coef(pown, w_own), 9)
    wait_all(6, gms.at[pl.ds(0, ns - 1)])
    t_m = inverse(unpack(jnp.sum(gms[...], axis=0), size), size)
    bulk_last()
    wait_all(4, puc.at[:, :, pl.ds(0, nc - 1)])
    for s in range(ns):
        for h in range(halves):
            for c in range(nc):
                pud[s * halves + h, c * kd : (c + 1) * kd, :] = puc[s, h, c]
    wait_all(8, ag.at[0, pl.ds(0, own * (ns - 1)), :])
    coef = summed_coef(0, 9)
    bulk_finish()
    reorthogonalise(0, ag[0], coef, None, 10)
    first_u, mine_u, norm_u1, norm_v1, scale_v1 = data_side(0, 10, 11, None)

    adjoint(mine_u, 1, 12)
    part = wpart[1]
    coef = panel_coef(pfull, part)
    share_coef(1, put_lane(coef, size, total(rbuf[0] * part) * scale_v1), 13)
    gather(1, 12, 14)
    coef = summed_coef(1, 13)
    along = rbuf[0] * (lane(coef, size) * scale_v1)
    wait_all(14, ag.at[1, pl.ds(0, own * (ns - 1)), :])
    reorthogonalise(1, ag[1], coef, along, 15)
    second_u, mine_u, norm_u2, norm_v2, scale_v2 = data_side(1, 15, 16, first_u)

    out_v[...] = rbuf[1] * (scale_v2 * math.sqrt(total_cols))
    for h in range(halves):
        out_u[h : h + 1, :] = mine_u[h] * math.sqrt(total_rows)
    row = jnp.zeros((1, LANES), F32)
    row = put_lane(row, 0, norm_v1 / math.sqrt(total_cols))
    row = put_lane(row, 1, norm_u1 / math.sqrt(total_rows))
    row = put_lane(row, 2, norm_v2 / math.sqrt(total_cols))
    row = put_lane(row, 3, norm_u2 / math.sqrt(total_rows))
    out_b[...] = row

    for copy in bulk.values():
        copy.wait_send()
    for index, span in drains:
        pltpu.make_async_copy(span, span, send.at[index]).wait()


def solution(mesh):
    nc, ns = mesh.shape["cell"], mesh.shape["station"]

    def per_device(sensitivity, tile_mask, data_panel, model_panel):
        rows, cols = sensitivity.shape
        kd, km = data_panel.shape[0], model_panel.shape[0]
        size = kd * nc
        tiles, halves = cols // LANES, rows // LANES
        own = tiles // ns
        vmem = pl.BlockSpec(memory_space=pltpu.VMEM)
        data_vector, model_vector, bidiag = pl.pallas_call(
            functools.partial(kernel, nc, ns, rows * ns, cols * nc),
            out_shape=(
                jax.ShapeDtypeStruct((halves, LANES), F32),
                jax.ShapeDtypeStruct((tiles, LANES), F32),
                jax.ShapeDtypeStruct((1, LANES), F32),
            ),
            in_specs=[pl.BlockSpec(memory_space=pltpu.HBM)] * 4,
            out_specs=(vmem, vmem, vmem),
            scratch_shapes=[
                pltpu.VMEM((ns, rows, cols // ns), F32),
                pltpu.VMEM((size, tiles, LANES), F32),
                pltpu.VMEM((size, own, LANES), F32),
                pltpu.VMEM((km, cols), F32),
                pltpu.SMEM(tile_mask.shape, jnp.int32),
                pltpu.VMEM(data_panel.shape, F32),
                pltpu.VMEM((halves, kd, LANES), F32),
                pltpu.VMEM((nc, halves, kd, LANES), F32),
                pltpu.VMEM((ns, halves, kd, LANES), F32),
                pltpu.VMEM((ns, halves, nc, kd, LANES), F32),
                pltpu.VMEM((ns * halves, size, LANES), F32),
                pltpu.VMEM((ns, size // 4, LANES), F32),
                pltpu.VMEM((nc, size // 4, LANES), F32),
                pltpu.VMEM((ns, size // 4, LANES), F32),
                pltpu.VMEM((2, tiles, LANES), F32),
                pltpu.VMEM((2, ns, own, LANES), F32),
                pltpu.VMEM((2, tiles, LANES), F32),
                pltpu.VMEM((2, nc * ns, 1, LANES), F32),
                pltpu.VMEM((2, tiles, LANES), F32),
                pltpu.VMEM((2, nc, 1, LANES), F32),
                pltpu.VMEM((2, nc * ns, halves, LANES), F32),
                pltpu.VMEM((ns * halves, LANES), F32),
                pltpu.VMEM((rows, LANES), F32),
                pltpu.VMEM((size, 8, LANES), F32),
                pltpu.VMEM((own, 8, LANES), F32),
                pltpu.VMEM((size, LANES), F32),
                pltpu.SemaphoreType.DMA((ns + 3,)),
                pltpu.SemaphoreType.DMA((17,)),
                pltpu.SemaphoreType.DMA((17,)),
                pltpu.SemaphoreType.DMA((9,)),
                pltpu.SemaphoreType.DMA((9,)),
            ],
            compiler_params=pltpu.CompilerParams(
                collective_id=0, has_side_effects=True, vmem_limit_bytes=48 * 1024 * 1024
            ),
            name="bidiagonalise",
        )(sensitivity, tile_mask, data_panel, model_panel)
        return data_vector.reshape(rows), model_vector.reshape(cols), bidiag[0, :4]

    return jax.shard_map(
        per_device,
        mesh=mesh,
        in_specs=(P("station", "cell"), P("station", "cell"), P("cell", "station"), P("station", "cell")),
        out_specs=(P("station"), P("cell"), P()),
        check_vma=False,
    )
```
